1024 devices in a mesh: expert: 16 (over z), etp: 4 (over x), dp: 16 (over y, core).
Axes of the slice: x: 4, y: 8, z: 16, core: 2. Of those that a mesh axis runs over, the one named last changes fastest.
Arguments:
- tokens: bfloat16 [1024, 6144], P('expert', 'dp'), may hold values from -6 to 6
- routes: int32 [1024, 4], P('expert'), may hold values from 0 to 15, all different within a row; in each aligned block of 64 rows (0 to 63, 64 to 127, ...) at most 21 rows name the same one
- combine_weights: float32 [1024, 4], P('expert'), may hold values from 0.2 to 1
- gate_weight: bfloat16 [16, 6144, 2688], P('expert', 'dp', 'etp'), may hold values from -0.078125 to 0.078125
- up_weight: bfloat16 [16, 6144, 2688], P('expert', 'dp', 'etp'), may hold values from -0.078125 to 0.078125
- down_weight: bfloat16 [16, 2688, 6144], P('expert', 'etp', 'dp'), may hold values from -0.125 to 0.125
- out_cotangent: bfloat16 [1024, 6144], P('expert', 'dp'), may hold values from -6 to 6
Outputs:
- layer_output: bfloat16 [1024, 6144], P('expert', ('dp', 'etp'))
- tokens_grad: bfloat16 [1024, 6144], P('expert', ('dp', 'etp'))
- gate_grad: bfloat16 [16, 6144, 2688], P('expert', 'dp', 'etp')
- up_grad: bfloat16 [16, 6144, 2688], P('expert', 'dp', 'etp')
- down_grad: bfloat16 [16, 2688, 6144], P('expert', 'etp', 'dp')
The draws below stay inside these ranges and needn't reach their ends.
Inputs may be any that keep to these rules, and one draw needn't show every extreme that they name: `routes`: A token names 4 different experts. Among the tokens of one block of 64, no expert is named by more than 21 tokens, and in every draw some block names some expert exactly 21 times; every expert is named somewhere.
All inputs are finite; a program needn't handle non-finite values.
Results may differ from the reference program's by a relative error of at most 0.038.
Values may be sent and summed in bfloat16 or wider, within the bound.
No kernel may reach another device: no remote copies, remote signals or barrier semaphores. Data moves between devices by JAX's collectives and lax.ppermute only.
A program may use at most 32 MiB of HBM per device.

```python
import math
import jax
import jax.numpy as jnp
import numpy as np
from jax import lax

D = 6144
FF = 2688
TOP = 4
TOK_BLK = 64
EXPERTS = 16
CAP = 21
TOKENS = 1024
SLOTS = 336
N_DP = 16


def block_scale(rng, dims, pieces, smallest, largest):
    def one(dim, shards_of):
        draws = jax.random.uniform(jax.random.fold_in(jax.random.fold_in(rng, 6), dim), (shards_of,), jnp.float32, smallest / len(pieces), largest / len(pieces))
        return jnp.repeat(jnp.exp(draws), dims[dim] // shards_of).reshape((-1,) + (1,) * (len(dims) - dim - 1))

    factor_of = one(*pieces[0])
    for cut in pieces[1:]:
        factor_of = factor_of * one(*cut)
    return factor_of


def shared_out(key, own, number, rows, amount, top, reach, skew):
    order = jax.random.permutation(key, amount)
    packed, common = load_shares(amount, rows * top, reach, skew, True), load_shares(amount, rows * top, reach, skew, False)
    places = jnp.arange(amount)

    def named(sizes, turn):
        used = int((sizes > 0).sum())
        fixed = max(1, used // 4)
        shifted = fixed + (places - fixed + turn * (used - fixed)) % max(1, amount - fixed)
        return jnp.zeros((amount,), jnp.int32).at[order[jnp.where(places < fixed, places, shifted)]].set(jnp.asarray(sizes, jnp.int32))

    sizes = jnp.where(number % 4 == 0, named(packed, number // 4), named(common, number - number // 4 - 1))
    mixed = jax.random.permutation(jax.random.fold_in(own, 3), amount)
    giver, sink = mixed[0:amount // 2 * 2:2], mixed[1:amount // 2 * 2:2]
    slack = jnp.minimum(sizes[giver] - 1, reach - sizes[sink]) // 2
    slack = jnp.where((giver == order[0]) | (sink == order[0]) | (sizes[sink] == 0), 0, jnp.maximum(slack, 0))
    shifted = jax.random.randint(jax.random.fold_in(own, 4), (amount // 2,), 0, 1 << 20) % (slack + 1)
    sizes = sizes.at[giver].add(-shifted).at[sink].add(shifted)
    labels = jnp.searchsorted(jnp.cumsum(sizes), jnp.arange(rows * top), side="right").astype(jnp.int32)
    listing = labels.reshape(top, rows).T
    listing = listing[jax.random.permutation(jax.random.fold_in(own, 1), rows)]
    turn = jax.random.randint(jax.random.fold_in(own, 2), (rows, 1), 0, top)
    return jnp.take_along_axis(listing, (jnp.arange(top)[None, :] + turn) % top, axis=1)


def load_shares(count, total, limit, skew, full):
    loads = [(1 << 20) // math.isqrt(standing ** skew) + 1 for standing in range(1, count + 1)]
    largest = limit if full else min(limit, max(-(-total // count), total * loads[0] // sum(loads)))
    least = 1 if total - largest >= count - 1 else 0
    counts, rest = [largest] + [least] * (count - 1), total - largest - least * (count - 1)
    while rest > 0:
        free = [i for i in range(1, count) if counts[i] < largest] or [i for i in range(1, count) if counts[i] < limit]
        whole, left = sum([loads[i] for i in free]), rest
        for i in free:
            more = min(limit - counts[i], max(1, left * loads[i] // whole), rest)
            counts[i] = counts[i] + more
            rest = rest - more
    return np.array(counts)


def normal_values(key, shape, scale, limit, cuts=(), held_as=jnp.bfloat16):
    level = block_scale(key, shape, cuts, -0.22, 0.18) if cuts else 1.0
    entries = jax.random.normal(key, shape, jnp.float32) * scale * level
    return jnp.minimum(jnp.maximum(entries, -limit), limit).astype(held_as)


def setup_inputs(seed: int = 0) -> dict:
    keys = jax.random.split(jax.random.key(seed), 8)
    tokens = normal_values(keys[0], (TOKENS, D), 1.0, 6.0, ((0, 16), (1, 16)))
    routes_keys = jax.random.split(jax.random.fold_in(keys[1], 1), TOKENS // TOK_BLK)
    routes_turns = jax.random.permutation(jax.random.fold_in(keys[1], 3), TOKENS // TOK_BLK)
    routes = jax.vmap(lambda own, number: shared_out(jax.random.fold_in(keys[1], 2), own, number, TOK_BLK, EXPERTS, TOP, CAP, 2))(routes_keys, routes_turns).reshape((TOKENS, TOP))
    combine_weights = jnp.clip(0.2 + 0.8 * jax.random.uniform(keys[2], (TOKENS, TOP), jnp.float32) ** block_scale(keys[2], (TOKENS, TOP), ((0, 16),), -0.2, 0.2), 0.2, 1.0)
    gate_weight = normal_values(keys[3], (EXPERTS, D, FF), D ** -0.5, 0.078125, ((0, 16), (1, 16), (2, 4)))
    up_weight = normal_values(keys[4], (EXPERTS, D, FF), D ** -0.5, 0.078125, ((0, 16), (1, 16), (2, 4)))
    down_weight = normal_values(keys[5], (EXPERTS, FF, D), FF ** -0.5, 0.125, ((0, 16), (1, 4), (2, 16)))
    out_cotangent = normal_values(keys[6], (TOKENS, D), 1.0, 6.0, ((0, 16), (1, 16)))
    return {"tokens": tokens, "routes": routes, "combine_weights": combine_weights, "gate_weight": gate_weight, "up_weight": up_weight, "down_weight": down_weight, "out_cotangent": out_cotangent}


def split_sum(left_side, right_side):
    slot_total = left_side.shape[0]
    grouped = left_side.reshape(slot_total, N_DP, -1).transpose(1, 0, 2).astype(jnp.float32)
    row_groups = right_side.reshape(N_DP, -1, right_side.shape[1]).astype(jnp.float32)
    partials = jnp.einsum('dsk,dkf->dsf', grouped, row_groups)
    rounded = lax.optimization_barrier(partials.astype(jnp.bfloat16))
    return jnp.sum(rounded.astype(jnp.float32), axis=0)


def slot_table(routes):
    block_count = TOKENS // TOK_BLK
    flat_ids = routes.reshape(block_count, TOK_BLK * TOP)
    hit_table = (flat_ids[:, :, None] == jnp.arange(EXPERTS, dtype=jnp.int32)[None, None, :]).astype(jnp.int32)
    before = jnp.cumsum(hit_table, axis=1) - hit_table
    rank_in_block = jnp.sum(before * hit_table, axis=2)
    block_index = jnp.arange(block_count, dtype=jnp.int32)[:, None]
    return (block_index * CAP + rank_in_block).reshape(TOKENS, TOP).astype(jnp.int32)


def expert_pass(operands):
    x_piece, grad_piece, weight_gate, weight_up, weight_down = operands
    gate_sum = split_sum(x_piece, weight_gate)
    up_sum = split_sum(x_piece, weight_up)
    hidden = (jax.nn.silu(gate_sum) * up_sum).astype(jnp.bfloat16)
    y_slot = jnp.dot(hidden, weight_down, preferred_element_type=jnp.float32).astype(jnp.bfloat16)
    d_hidden = split_sum(grad_piece, weight_down.T)
    sigmoid_gate = jax.nn.sigmoid(gate_sum)
    d_up = (d_hidden * gate_sum * sigmoid_gate).astype(jnp.bfloat16)
    d_gate = (d_hidden * up_sum * sigmoid_gate * (1.0 + gate_sum * (1.0 - sigmoid_gate))).astype(jnp.bfloat16)
    down_grad = jnp.dot(hidden.T, grad_piece, preferred_element_type=jnp.float32).astype(jnp.bfloat16)
    gate_grad = jnp.dot(x_piece.T, d_gate, preferred_element_type=jnp.float32).astype(jnp.bfloat16)
    up_grad = jnp.dot(x_piece.T, d_up, preferred_element_type=jnp.float32).astype(jnp.bfloat16)
    dx_total = jnp.dot(d_gate, weight_gate.T, preferred_element_type=jnp.float32) + jnp.dot(d_up, weight_up.T, preferred_element_type=jnp.float32)
    return y_slot, dx_total.astype(jnp.bfloat16), gate_grad, up_grad, down_grad


def reference(tokens, routes, combine_weights, gate_weight, up_weight, down_weight, out_cotangent):
    slot_index = slot_table(routes)
    token_rows = jnp.broadcast_to(tokens[:, None, :], (TOKENS, TOP, D))
    scaled_rows = (combine_weights[:, :, None] * out_cotangent[:, None, :].astype(jnp.float32)).astype(jnp.bfloat16)
    x_slots = jnp.zeros((EXPERTS, SLOTS, D), jnp.bfloat16).at[routes, slot_index].set(token_rows)
    g_slots = jnp.zeros((EXPERTS, SLOTS, D), jnp.bfloat16).at[routes, slot_index].set(scaled_rows)
    y_slots, dx_slots, gate_grad, up_grad, down_grad = lax.map(expert_pass, (x_slots, g_slots, gate_weight, up_weight, down_weight))
    y_chosen = y_slots[routes, slot_index].astype(jnp.float32)
    dx_chosen = dx_slots[routes, slot_index].astype(jnp.float32)
    layer_output = jnp.sum(combine_weights[:, :, None] * y_chosen, axis=1).astype(jnp.bfloat16)
    tokens_grad = jnp.sum(dx_chosen, axis=1).astype(jnp.bfloat16)
    return layer_output, tokens_grad, gate_grad, up_grad, down_grad
```

```python
import jax
import jax.numpy as jnp
from jax import lax
from jax.sharding import PartitionSpec as P

PAD_CAP = 24
LANES = 128
f32 = jnp.float32
bf16 = jnp.bfloat16


def mm(left, right, dims):
    return lax.dot_general(left, right, (dims, ((), ())), preferred_element_type=f32)


def swap(x, axis, groups=None):
    return lax.all_to_all(
        x, axis, split_axis=0, concat_axis=0, tiled=True, axis_index_groups=groups
    )


def widen(x, width):
    return jnp.pad(x, ((0, 0), (0, width - x.shape[1])))


def local(tokens, routes, combine_weights, gate_weight, up_weight, down_weight, out_cotangent):
    block_len, top_count = routes.shape
    n_exp = lax.axis_size("expert")
    n_etp = lax.axis_size("etp")
    n_dp = lax.axis_size("dp")
    n_y = n_dp // 2
    width = tokens.shape[1]
    piece = width // n_etp
    hid = gate_weight.shape[2]
    slots = n_exp * PAD_CAP
    same_core = [[2 * y + c for y in range(n_y)] for c in range(2)]
    same_chip = [[2 * y, 2 * y + 1] for y in range(n_y)]
    col = lax.axis_index("etp") * piece

    slot = lax.broadcasted_iota(jnp.int32, (block_len, slots), 1)
    owner = slot // PAD_CAP
    rank = slot % PAD_CAP
    hit = owner == routes[:, 0:1]
    weight = jnp.where(hit, combine_weights[:, 0:1], 0.0)
    for k in range(1, top_count):
        hit_k = owner == routes[:, k : k + 1]
        weight = jnp.where(hit_k, combine_weights[:, k : k + 1], weight)
        hit = hit | hit_k
    earlier = (
        lax.broadcasted_iota(jnp.int32, (block_len, block_len), 1)
        < lax.broadcasted_iota(jnp.int32, (block_len, block_len), 0)
    ).astype(bf16)
    before = mm(earlier, hit.astype(bf16), ((1,), (0,)))
    place = hit & (before == rank.astype(f32))
    weight = jnp.where(place, weight, 0.0)
    place_bf = place.astype(bf16)

    tok = lax.dynamic_slice_in_dim(tokens, col, piece, 1)
    cot = lax.dynamic_slice_in_dim(out_cotangent, col, piece, 1)
    both = mm(place_bf, jnp.concatenate([widen(tok, LANES), widen(cot, LANES)], 1), ((0,), (0,)))
    slot_weight = jnp.sum(weight, axis=0)[:, None]
    scale = jnp.where(
        lax.broadcasted_iota(jnp.int32, (slots, 2 * LANES), 1) < LANES, 1.0, slot_weight
    )
    send = (both * scale).astype(bf16).reshape(n_exp, PAD_CAP, 2 * LANES)
    got = swap(send, "expert").reshape(1, slots, 2 * LANES)
    pieces = swap(jnp.broadcast_to(got, (n_etp, slots, 2 * LANES)), "etp")
    x = jnp.concatenate([pieces[i, :, :piece] for i in range(n_etp)], axis=1)
    g = jnp.concatenate([pieces[i, :, LANES : LANES + piece] for i in range(n_etp)], axis=1)

    w_gate, w_up, w_down = gate_weight[0], up_weight[0], down_weight[0]
    part = jnp.concatenate(
        [
            mm(x, w_gate, ((1,), (0,))).astype(bf16),
            mm(x, w_up, ((1,), (0,))).astype(bf16),
            mm(g, w_down, ((1,), (1,))).astype(bf16),
        ],
        axis=1,
    ).reshape(2, slots // 2, 3 * hid)
    chip = swap(part, "dp", same_chip).astype(f32)
    chip = (chip[0] + chip[1]).astype(bf16).reshape(n_y, PAD_CAP, 3 * hid)
    total = jnp.sum(swap(chip, "dp", same_core).astype(f32), axis=0)
    gate, up, d_hidden = total[:, :hid], total[:, hid : 2 * hid], total[:, 2 * hid :]
    sig = jax.nn.sigmoid(gate)
    act = jnp.concatenate(
        [
            (gate * sig * up).astype(bf16),
            (d_hidden * up * sig * (1.0 + gate * (1.0 - sig))).astype(bf16),
            (d_hidden * gate * sig).astype(bf16),
        ],
        axis=1,
    )
    half = lax.all_gather(act, "dp", axis=0, tiled=True, axis_index_groups=same_core)
    full = swap(
        jnp.broadcast_to(half[None], (2, slots // 2, 3 * hid)), "dp", same_chip
    ).reshape(slots, 3 * hid)
    hidden, d_gate, d_up = full[:, :hid], full[:, hid : 2 * hid], full[:, 2 * hid :]

    y = mm(hidden, w_down, ((1,), (0,))).astype(bf16)
    dx = (mm(d_gate, w_gate, ((1,), (1,))) + mm(d_up, w_up, ((1,), (1,)))).astype(bf16)
    out = jnp.stack(
        [
            jnp.concatenate(
                [
                    widen(y[:, i * piece : (i + 1) * piece], LANES),
                    widen(dx[:, i * piece : (i + 1) * piece], LANES),
                ],
                axis=1,
            )
            for i in range(n_etp)
        ]
    )
    out = jnp.sum(swap(out, "etp").astype(f32), axis=0).astype(bf16)
    back = swap(out.reshape(n_exp, PAD_CAP, 2 * LANES), "expert").reshape(slots, 2 * LANES)
    down_grad = mm(hidden, g, ((0,), (0,))).astype(bf16)
    gate_grad = mm(x, d_gate, ((0,), (0,))).astype(bf16)
    up_grad = mm(x, d_up, ((0,), (0,))).astype(bf16)
    layer_output = jnp.dot(
        weight, back[:, :piece].astype(f32), precision=lax.Precision.HIGHEST
    ).astype(bf16)
    tokens_grad = mm(place_bf, back[:, LANES : LANES + piece], ((1,), (0,))).astype(bf16)
    return layer_output, tokens_grad, gate_grad[None], up_grad[None], down_grad[None]


def solution(mesh):
    placed = (
        P("expert", "dp"),
        P("expert", None),
        P("expert", None),
        P("expert", "dp", "etp"),
        P("expert", "dp", "etp"),
        P("expert", "etp", "dp"),
        P("expert", "dp"),
    )
    return jax.shard_map(
        local,
        mesh=mesh,
        in_specs=placed,
        out_specs=(
            P("expert", ("dp", "etp")),
            P("expert", ("dp", "etp")),
            P("expert", "dp", "etp"),
            P("expert", "dp", "etp"),
            P("expert", "etp", "dp"),
        ),
        check_vma=False,
    )
```

```python
import functools

import jax
import jax.numpy as jnp
from jax import lax
from jax.experimental import pallas as pl
from jax.experimental.pallas import tpu as pltpu
from jax.sharding import PartitionSpec as P

PAD_CAP = 24
LANES = 128
f32 = jnp.float32
bf16 = jnp.bfloat16


def mm(left, right, dims):
    return lax.dot_general(left, right, (dims, ((), ())), preferred_element_type=f32)


def swap(x, axis, groups=None):
    return lax.all_to_all(
        x, axis, split_axis=0, concat_axis=0, tiled=True, axis_index_groups=groups
    )


def call(kernel, out_shapes, flops, n_scalar, *args, far=False, scratch=(), room=12):
    smem = pl.BlockSpec(memory_space=pltpu.SMEM)
    vmem = pl.BlockSpec(memory_space=pltpu.VMEM)
    held = pl.BlockSpec(memory_space=pltpu.HBM) if far else vmem
    moved = sum(a.size * a.dtype.itemsize for a in args) + sum(
        o.size * o.dtype.itemsize for o in out_shapes
    )
    return pl.pallas_call(
        kernel,
        out_shape=out_shapes,
        in_specs=[smem] * n_scalar + [held] * (len(args) - n_scalar),
        out_specs=[vmem] * len(out_shapes),
        scratch_shapes=list(scratch),
        compiler_params=pltpu.CompilerParams(vmem_limit_bytes=room * 1024 * 1024),
        cost_estimate=pl.CostEstimate(flops=flops, bytes_accessed=moved, transcendentals=0),
    )(*args)


def dispatch_kernel(
    piece, col_ref, tok_hbm, cot_hbm, route_hbm, cw_hbm, send_ref, place_ref, weight_ref,
    tok_ref, cot_ref, route_ref, cw_ref, sems,
):
    pairs = ((route_hbm, route_ref), (cw_hbm, cw_ref), (tok_hbm, tok_ref), (cot_hbm, cot_ref))
    copies = [pltpu.make_async_copy(a, b, sems.at[i]) for i, (a, b) in enumerate(pairs)]
    for copy in copies:
        copy.start()
    copies[0].wait()
    copies[1].wait()
    width = tok_ref.shape[1]
    top_count, block_len = route_ref.shape
    slots = send_ref.shape[0]
    slot = lax.broadcasted_iota(jnp.int32, (slots, block_len), 0)
    owner = lax.shift_right_logical(slot * 2731, 16)
    rank = slot - owner * PAD_CAP
    hit = jnp.zeros((slots, block_len), f32)
    weight = jnp.zeros((slots, block_len), f32)
    for k in range(top_count):
        hit_k = owner == route_ref[k : k + 1, :]
        hit = jnp.where(hit_k, 1.0, hit)
        weight = jnp.where(hit_k, cw_ref[k : k + 1, :], weight)
    earlier = (
        lax.broadcasted_iota(jnp.int32, (block_len, block_len), 0)
        < lax.broadcasted_iota(jnp.int32, (block_len, block_len), 1)
    )
    earlier = jnp.where(earlier, 1.0, 0.0).astype(bf16)
    before = mm(hit.astype(bf16), earlier, ((1,), (0,)))
    place = jnp.where(before == rank.astype(f32), hit, 0.0)
    weight = weight * place
    place_bf = place.astype(bf16)
    place_ref[...] = place_bf
    weight_ref[...] = weight
    lane = lax.broadcasted_iota(jnp.int32, (width, LANES), 1)
    row = lax.broadcasted_iota(jnp.int32, (width, LANES), 0)
    pick = jnp.where((row == lane + col_ref[0]) & (lane < piece), 1.0, 0.0).astype(bf16)
    copies[2].wait()
    copies[3].wait()
    tok = mm(tok_ref[...], pick, ((1,), (0,))).astype(bf16)
    cot = mm(cot_ref[...], pick, ((1,), (0,))).astype(bf16)
    send_ref[:, :LANES] = mm(place_bf, tok, ((1,), (0,))).astype(bf16)
    slot_weight = jnp.sum(weight, axis=1, keepdims=True)
    send_ref[:, LANES:] = (mm(place_bf, cot, ((1,), (0,))) * slot_weight).astype(bf16)


def front_kernel(
    piece, half_ref, piece_ref, gate_ref, up_ref, down_ref, part_ref, x_ref, g_ref
):
    rows = part_ref.shape[0]
    hid = gate_ref.shape[0]
    at = pl.ds(pl.multiple_of(half_ref[0] * rows, 16), rows)
    n_etp = piece_ref.shape[0]
    x = jnp.concatenate([piece_ref[i, at, 0:piece] for i in range(n_etp)], axis=1)
    g = jnp.concatenate(
        [piece_ref[i, at, LANES : LANES + piece] for i in range(n_etp)], axis=1
    )
    x_ref[...] = x
    g_ref[...] = g
    ends = (0, hid, 2 * hid, 3 * hid)
    for lo in range(0, 3 * hid, 256):
        hi = min(lo + 256, 3 * hid)
        total = None
        for left, first in ((x, 0), (g, 2)):
            rights, filled = [], False
            for j, ref in enumerate((gate_ref, up_ref, down_ref)):
                a, b = max(lo, ends[j]), min(hi, ends[j + 1])
                if a >= b:
                    continue
                if (j == 2) == (first == 2):
                    rights.append(ref[a - ends[j] : b - ends[j], :])
                    filled = True
                else:
                    rights.append(jnp.zeros((b - a, ref.shape[1]), bf16))
            if not filled:
                continue
            right = rights[0] if len(rights) == 1 else jnp.concatenate(rights, axis=0)
            term = mm(left, right, ((1,), (1,)))
            total = term if total is None else total + term
        part_ref[:, lo:hi] = total.astype(bf16)


def combine_kernel(piece, weight_ref, place_ref, back_ref, out_ref, grad_ref):
    back = back_ref[...]
    rest = weight_ref[...]
    total = None
    for _ in range(3):
        high = rest.astype(bf16)
        rest = rest - high.astype(f32)
        term = mm(high, back, ((0,), (0,)))
        total = term if total is None else total + term
    out_ref[...] = total[:, :piece].astype(bf16)
    grad_ref[...] = mm(place_ref[...], back, ((0,), (0,)))[:, piece : 2 * piece].astype(bf16)


def local(tokens, routes, combine_weights, gate_weight, up_weight, down_weight, out_cotangent):
    block_len, top_count = routes.shape
    n_exp = lax.axis_size("expert")
    n_etp = lax.axis_size("etp")
    n_dp = lax.axis_size("dp")
    n_y = n_dp // 2
    width = tokens.shape[1]
    piece = width // n_etp
    hid = gate_weight.shape[2]
    slots = n_exp * PAD_CAP
    same_core = [[2 * y + c for y in range(n_y)] for c in range(2)]
    same_chip = [[2 * y, 2 * y + 1] for y in range(n_y)]
    core = lax.bitwise_and(lax.axis_index("dp"), 1)
    col = lax.axis_index("etp") * piece

    send, place, weight = call(
        functools.partial(dispatch_kernel, piece),
        [
            jax.ShapeDtypeStruct((slots, 2 * LANES), bf16),
            jax.ShapeDtypeStruct((slots, block_len), bf16),
            jax.ShapeDtypeStruct((slots, block_len), f32),
        ],
        50_000_000,
        1,
        col[None],
        tokens,
        out_cotangent,
        routes.T,
        combine_weights.T,
        far=True,
        room=60,
        scratch=[
            pltpu.VMEM(tokens.shape, bf16),
            pltpu.VMEM(out_cotangent.shape, bf16),
            pltpu.VMEM((top_count, block_len), jnp.int32),
            pltpu.VMEM((top_count, block_len), f32),
            pltpu.SemaphoreType.DMA((4,)),
        ],
    )
    got = swap(send.reshape(n_exp, PAD_CAP, 2 * LANES), "expert").reshape(1, slots, 2 * LANES)
    pieces = swap(jnp.broadcast_to(got, (n_etp, slots, 2 * LANES)), "etp")

    w_gate, w_up, w_down = gate_weight[0].T, up_weight[0].T, down_weight[0]

    def front(which):
        return call(
            functools.partial(front_kernel, piece),
            [
                jax.ShapeDtypeStruct((slots // 2, 3 * hid), bf16),
                jax.ShapeDtypeStruct((slots // 2, width), bf16),
                jax.ShapeDtypeStruct((slots // 2, width), bf16),
            ],
            3 * slots * width * hid,
            1,
            which[None],
            pieces,
            w_gate,
            w_up,
            w_down,
        )

    theirs, x_theirs, g_theirs = front(1 - core)
    theirs = lax.ppermute(theirs, "dp", [(i, i ^ 1) for i in range(n_dp)])
    mine, x_mine, g_mine = front(core)
    chip = (mine.astype(f32) + theirs.astype(f32)).astype(bf16).reshape(n_y, PAD_CAP, 3 * hid)
    total = jnp.sum(swap(chip, "dp", same_core).astype(f32), axis=0)
    gate, up, d_hidden = total[:, :hid], total[:, hid : 2 * hid], total[:, 2 * hid :]
    sig = jax.nn.sigmoid(gate)
    act = jnp.concatenate(
        [
            (gate * sig * up).astype(bf16),
            (d_hidden * up * sig * (1.0 + gate * (1.0 - sig))).astype(bf16),
            (d_hidden * gate * sig).astype(bf16),
        ],
        axis=1,
    )
    half = lax.all_gather(act, "dp", axis=0, tiled=True, axis_index_groups=same_core)
    full = swap(
        jnp.broadcast_to(half[None], (2, slots // 2, 3 * hid)), "dp", same_chip
    ).reshape(slots, 3 * hid)
    hidden, d_gate, d_up = full[:, :hid], full[:, hid : 2 * hid], full[:, 2 * hid :]

    y = mm(hidden, w_down, ((1,), (0,))).astype(bf16)
    dx = (mm(d_gate, w_gate, ((1,), (0,))) + mm(d_up, w_up, ((1,), (0,)))).astype(bf16)
    out = jnp.concatenate(
        [y.T.reshape(n_etp, piece, slots), dx.T.reshape(n_etp, piece, slots)], axis=1
    )
    out = jnp.sum(swap(out, "etp").astype(f32), axis=0).astype(bf16).T
    back = swap(out.reshape(n_exp, PAD_CAP, 2 * piece), "expert").reshape(slots, 2 * piece)

    def in_order(own, other):
        first = core == 0
        return jnp.concatenate(
            [jnp.where(first, own, other), jnp.where(first, other, own)], axis=0
        )

    x = in_order(x_mine, x_theirs)
    g = in_order(g_mine, g_theirs)
    down_grad = mm(hidden, g, ((0,), (0,))).astype(bf16)
    gate_grad = mm(x, d_gate, ((0,), (0,))).astype(bf16)
    up_grad = mm(x, d_up, ((0,), (0,))).astype(bf16)
    layer_output, tokens_grad = call(
        functools.partial(combine_kernel, piece),
        [
            jax.ShapeDtypeStruct((block_len, piece), bf16),
            jax.ShapeDtypeStruct((block_len, piece), bf16),
        ],
        40_000_000,
        0,
        weight,
        place,
        back,
    )
    return layer_output, tokens_grad, gate_grad[None], up_grad[None], down_grad[None]


def solution(mesh):
    placed = (
        P("expert", "dp"),
        P("expert", None),
        P("expert", None),
        P("expert", "dp", "etp"),
        P("expert", "dp", "etp"),
        P("expert", "etp", "dp"),
        P("expert", "dp"),
    )
    return jax.shard_map(
        local,
        mesh=mesh,
        in_specs=placed,
        out_specs=(
            P("expert", ("dp", "etp")),
            P("expert", ("dp", "etp")),
            P("expert", "dp", "etp"),
            P("expert", "dp", "etp"),
            P("expert", "etp", "dp"),
        ),
        check_vma=False,
    )
```

```python
import functools

import jax
import jax.numpy as jnp
from jax import lax
from jax.experimental import pallas as pl
from jax.experimental.pallas import tpu as pltpu
from jax.sharding import PartitionSpec as P

LANES = 128
f32 = jnp.float32
bf16 = jnp.bfloat16


def mm(left, right, dims):
    return lax.dot_general(left, right, (dims, ((), ())), preferred_element_type=f32)


def swap(x, axis, groups=None):
    return lax.all_to_all(
        x, axis, split_axis=0, concat_axis=0, tiled=True, axis_index_groups=groups
    )


def iota(shape, axis):
    return lax.broadcasted_iota(jnp.int32, shape, axis)


def call(kernel, outs, flops, n_scalar, *args, far=False, scratch=(), room=16):
    smem = pl.BlockSpec(memory_space=pltpu.SMEM)
    vmem = pl.BlockSpec(memory_space=pltpu.VMEM)
    held = pl.BlockSpec(memory_space=pltpu.HBM) if far else vmem
    outs = [jax.ShapeDtypeStruct(*o) for o in outs]
    moved = sum(a.size * a.dtype.itemsize for a in (*args, *outs))
    return pl.pallas_call(
        kernel,
        out_shape=outs,
        in_specs=[smem] * n_scalar + [held] * (len(args) - n_scalar),
        out_specs=[vmem] * len(outs),
        scratch_shapes=list(scratch),
        compiler_params=pltpu.CompilerParams(vmem_limit_bytes=room * 1024 * 1024),
        cost_estimate=pl.CostEstimate(flops=flops, bytes_accessed=moved, transcendentals=0),
    )(*args)


CAP = 21
PACK = 32
FOLD = PACK - CAP


def dispatch_kernel(
    piece,
    col_ref,
    tok_hbm,
    cot_hbm,
    route_hbm,
    cw_hbm,
    send_ref,
    place_ref,
    place_b_ref,
    place_c_ref,
    weight_ref,
    tok_ref,
    cot_ref,
    route_ref,
    cw_ref,
    sems,
):
    pairs = ((route_hbm, route_ref), (cw_hbm, cw_ref), (tok_hbm, tok_ref), (cot_hbm, cot_ref))
    copies = [pltpu.make_async_copy(a, b, sems.at[i]) for i, (a, b) in enumerate(pairs)]
    for copy in copies:
        copy.start()
    copies[0].wait()
    copies[1].wait()
    width = tok_ref.shape[1]
    top_count, block_len = route_ref.shape
    rows = send_ref.shape[0]
    row = iota((rows, block_len), 0)
    owner = lax.shift_right_logical(row, 5)
    inner = row & (PACK - 1)
    hit = jnp.zeros((rows, block_len), f32)
    weight = jnp.zeros((rows, block_len), f32)
    for k in range(top_count):
        hit_k = owner == route_ref[k : k + 1, :]
        hit = jnp.where(hit_k, 1.0, hit)
        weight = jnp.where(hit_k, cw_ref[k : k + 1, :], weight)
    square = (block_len, block_len)
    earlier = jnp.where(iota(square, 0) < iota(square, 1), 1.0, 0.0).astype(bf16)
    before = mm(hit.astype(bf16), earlier, ((1,), (0,)))
    inner_f = inner.astype(f32)
    folded = jnp.where(inner >= CAP, hit, 0.0)
    place = jnp.where((before == inner_f) & (inner < CAP), hit, 0.0)
    place_b = jnp.where(before == inner_f - CAP, folded, 0.0)
    place_c = jnp.where(before == inner_f - (CAP - FOLD), folded, 0.0)
    place_ref[...] = place.astype(bf16)
    place_b_ref[...] = place_b.astype(bf16)
    place_c_ref[...] = place_c.astype(bf16)
    weight_ref[...] = weight * place
    pick_row = iota((width, LANES), 0) - col_ref[0]
    lane = iota((width, LANES), 1)
    pick_x = jnp.where((pick_row == lane) & (lane < piece), 1.0, 0.0).astype(bf16)
    pick_g = jnp.where((pick_row == lane - piece) & (lane >= piece), 1.0, 0.0).astype(bf16)
    rest = (lane & 63) + (LANES - piece)
    pick_r = jnp.where(pick_row == rest, 1.0, 0.0).astype(bf16)
    copies[2].wait()
    copies[3].wait()
    cot = cot_ref[...]
    first = mm(tok_ref[...], pick_x, ((1,), (0,))) + mm(cot, pick_g, ((1,), (0,)))
    last = mm(cot, pick_r, ((1,), (0,))).astype(bf16)
    lanes = iota((rows, LANES), 1)
    scale = jnp.sum(weight * place, axis=1, keepdims=True)
    scale_b = jnp.sum(weight * place_b, axis=1, keepdims=True)
    scale_c = jnp.sum(weight * place_c, axis=1, keepdims=True)
    a = mm(place.astype(bf16), first.astype(bf16), ((1,), (0,)))
    b = mm(place_b.astype(bf16), last, ((1,), (0,)))
    c = mm(place_c.astype(bf16), last, ((1,), (0,)))
    a = jnp.where(lanes < piece, a, a * scale)
    send_ref[...] = (a + jnp.where(lanes < 64, b * scale_b, c * scale_c)).astype(bf16)


def selectors(slots, rows, flip):
    shape, slot_axis = ((rows, slots), 1) if flip else ((slots, rows), 0)
    slot = iota(shape, slot_axis)
    row = iota(shape, 1 - slot_axis)
    base = lax.shift_right_logical(row, 5) * CAP
    inner = row & (PACK - 1)
    at = slot - base
    sel_a = jnp.where((at == inner) & (inner < CAP), 1.0, 0.0).astype(bf16)
    low = at == inner - CAP
    high = (at == inner - (CAP - FOLD)) & (inner < PACK - 1)
    sel_b = jnp.where((low | high) & (inner >= CAP), 1.0, 0.0).astype(bf16)
    return sel_a, sel_b


def is_low(slots, lanes):
    slot = iota((slots, lanes), 0)
    rank = slot - lax.shift_right_logical(slot * 3121, 16) * CAP
    return rank < FOLD


def partials(half_ref, xg, w_ref, part_ref):
    chunks = part_ref.shape[0]
    for j in range(0, chunks, 2):
        at = half_ref[0] * chunks + j
        w = jnp.concatenate([w_ref[at], w_ref[at + 1]], axis=0)
        got = mm(xg, w, ((1,), (1,))).astype(bf16)
        part_ref[j] = got[:, :LANES]
        part_ref[j + 1] = got[:, LANES:]


def first_kernel(piece, half_ref, pack_ref, w_ref, part_ref, xg_ref):
    n_etp, rows, _ = pack_ref.shape
    slots = part_ref.shape[1]
    sel_a, sel_b = selectors(slots, rows, False)
    packed = jnp.concatenate([pack_ref[i] for i in range(n_etp)], axis=1)
    a = mm(sel_a, packed, ((1,), (0,)))
    b = mm(sel_b, packed, ((1,), (0,)))
    low = is_low(slots, 64)
    parts_x, parts_g = [], []
    for i in range(n_etp):
        at = LANES * i
        parts_x.append(a[:, at : at + piece])
        parts_g.append(a[:, at + piece : at + LANES])
        parts_g.append(jnp.where(low, b[:, at : at + 64], b[:, at + 64 : at + LANES]))
    xg = jnp.concatenate(parts_x + parts_g, axis=1).astype(bf16)
    xg_ref[...] = xg
    partials(half_ref, xg, w_ref, part_ref)


def second_kernel(half_ref, xg_ref, w_ref, part_ref):
    partials(half_ref, xg_ref[...], w_ref, part_ref)


def act_kernel(unit, sum_ref, act_ref):
    total = sum_ref[0].astype(f32)
    for j in range(1, sum_ref.shape[0]):
        total = total + sum_ref[j].astype(f32)
    keep = iota(total.shape, 1) < unit
    gate = jnp.where(keep, total, 0.0)
    up = jnp.where(keep, pltpu.roll(total, LANES - unit, 1), 0.0)
    d_hidden = jnp.where(keep, pltpu.roll(total, LANES - 2 * unit, 1), 0.0)
    sig = jax.nn.sigmoid(gate)
    hidden = gate * sig * up
    d_gate = d_hidden * up * sig * (1.0 + gate * (1.0 - sig))
    d_up = d_hidden * gate * sig
    act_ref[...] = (
        hidden + pltpu.roll(d_gate, unit, 1) + pltpu.roll(d_up, 2 * unit, 1)
    ).astype(bf16)


def back_sum(half_ref, act_ref, w_ref):
    chunks = act_ref.shape[0]
    act = jnp.concatenate([act_ref[j] for j in range(chunks)], axis=1)
    w = w_ref[pl.ds(half_ref[0] * chunks, chunks)]
    return mm(act, w.reshape(chunks * LANES, w.shape[2]), ((1,), (0,)))


def back_kernel(half_ref, act_ref, w_ref, sum_ref):
    sum_ref[...] = back_sum(half_ref, act_ref, w_ref)


def pack_kernel(piece, half_ref, act_ref, w_ref, sum_ref, pack_ref):
    n_etp, rows, _ = pack_ref.shape
    slots, width = sum_ref.shape[0], sum_ref.shape[1] // 2
    total = (sum_ref[...] + back_sum(half_ref, act_ref, w_ref)).astype(bf16).astype(f32)
    sel_a, sel_b = selectors(slots, rows, True)
    low = is_low(slots, 64)
    for i in range(n_etp):
        y = total[:, piece * i : piece * (i + 1)]
        at = width + piece * i
        a = jnp.concatenate([y, total[:, at : at + LANES - piece]], axis=1).astype(bf16)
        tail = total[:, at + LANES - piece : at + piece]
        b = jnp.concatenate(
            [jnp.where(low, tail, 0.0), jnp.where(low, 0.0, tail)], axis=1
        ).astype(bf16)
        pack_ref[i] = (mm(sel_a, a, ((1,), (0,))) + mm(sel_b, b, ((1,), (0,)))).astype(bf16)


def combine_kernel(
    piece, weight_ref, place_ref, place_b_ref, place_c_ref, back_ref, out_ref, grad_ref
):
    back = back_ref[...]
    rest = weight_ref[...]
    total = None
    for _ in range(3):
        high = rest.astype(bf16)
        rest = rest - high.astype(f32)
        term = mm(high, back, ((0,), (0,)))
        total = term if total is None else total + term
    out_ref[...] = total[:, :piece].astype(bf16)
    a = mm(place_ref[...], back, ((0,), (0,)))
    b = mm(place_b_ref[...], back, ((0,), (0,)))
    c = mm(place_c_ref[...], back, ((0,), (0,)))
    grad_ref[...] = jnp.concatenate(
        [a[:, piece:LANES], b[:, :64] + c[:, 64:]], axis=1
    ).astype(bf16)


def local(tokens, routes, combine_weights, gate_weight, up_weight, down_weight, out_cotangent):
    block_len, top_count = routes.shape
    n_exp = lax.axis_size("expert")
    n_etp = lax.axis_size("etp")
    n_dp = lax.axis_size("dp")
    n_y = n_dp // 2
    width = tokens.shape[1]
    piece = width // n_etp
    hid = gate_weight.shape[2]
    unit = hid // n_dp
    slots = n_exp * CAP
    rows = n_exp * PACK
    same_core = [[2 * y + c for y in range(n_y)] for c in range(2)]
    other_core = [(i, i ^ 1) for i in range(n_dp)]
    core = lax.bitwise_and(lax.axis_index("dp"), 1)
    mine, theirs = core[None], (1 - core)[None]
    col = lax.axis_index("etp") * piece

    send, place, place_b, place_c, weight = call(
        functools.partial(dispatch_kernel, piece),
        [
            ((rows, LANES), bf16),
            ((rows, block_len), bf16),
            ((rows, block_len), bf16),
            ((rows, block_len), bf16),
            ((rows, block_len), f32),
        ],
        60_000_000,
        1,
        col[None],
        tokens,
        out_cotangent,
        routes.T,
        combine_weights.T,
        far=True,
        room=60,
        scratch=[
            pltpu.VMEM(tokens.shape, bf16),
            pltpu.VMEM(out_cotangent.shape, bf16),
            pltpu.VMEM((top_count, block_len), jnp.int32),
            pltpu.VMEM((top_count, block_len), f32),
            pltpu.SemaphoreType.DMA((4,)),
        ],
    )
    send, gate_weight, up_weight, down_weight = lax.optimization_barrier(
        (send, gate_weight, up_weight, down_weight)
    )
    w_gate = gate_weight[0].T.reshape(n_dp, unit, width)
    w_up = up_weight[0].T.reshape(n_dp, unit, width)
    w_down = down_weight[0].reshape(n_dp, unit, width)

    def zeros(n):
        return jnp.zeros((n_dp, n, width), bf16)

    spare = LANES - 3 * unit
    w_front = jnp.concatenate(
        [
            jnp.concatenate([w_gate, w_up, zeros(unit + spare)], axis=1),
            jnp.concatenate([zeros(2 * unit), w_down, zeros(spare)], axis=1),
        ],
        axis=2,
    )
    w_back = jnp.concatenate(
        [
            jnp.concatenate([w_down, zeros(2 * unit + spare)], axis=1),
            jnp.concatenate([zeros(unit), w_gate, w_up, zeros(spare)], axis=1),
        ],
        axis=2,
    )

    got = swap(send.reshape(n_exp, PACK, LANES), "expert").reshape(1, rows, LANES)
    packs = swap(jnp.broadcast_to(got, (n_etp, rows, LANES)), "etp")

    half_flops = 2 * slots * 2 * width * n_y * LANES
    part_shape = ((n_y, slots, LANES), bf16)
    part_theirs, xg = call(
        functools.partial(first_kernel, piece),
        [part_shape, ((slots, 2 * width), bf16)],
        2 * half_flops,
        1,
        theirs,
        packs,
        w_front,
    )
    arrived = lax.ppermute(part_theirs, "dp", other_core)
    (part_mine,) = call(second_kernel, [part_shape], half_flops, 1, mine, xg, w_front)
    chip = (part_mine.astype(f32) + arrived.astype(f32)).astype(bf16)
    (act,) = call(
        functools.partial(act_kernel, unit),
        [((slots, LANES), bf16)],
        10_000_000,
        0,
        swap(chip, "dp", same_core),
    )
    act_mine = lax.all_gather(act, "dp", axis=0, axis_index_groups=same_core)
    act_theirs = lax.ppermute(act_mine, "dp", other_core)
    (total,) = call(
        back_kernel, [((slots, 2 * width), f32)], half_flops, 1, mine, act_mine, w_back
    )
    (out,) = call(
        functools.partial(pack_kernel, piece),
        [((n_etp, rows, LANES), bf16)],
        2 * half_flops,
        1,
        theirs,
        act_theirs,
        w_back,
        total,
    )
    out = jnp.sum(swap(out, "etp").astype(f32), axis=0).astype(bf16)
    back = swap(out.reshape(n_exp, PACK, LANES), "expert").reshape(rows, LANES)

    grads = [mm(a, xg, ((1,), (0,))).astype(bf16) for a in (act_mine, act_theirs)]

    def take(start, at):
        own, other = (g[:, start : start + unit, at : at + width] for g in grads)
        first = core == 0
        ordered = jnp.concatenate(
            [jnp.where(first, own, other), jnp.where(first, other, own)], axis=0
        )
        return ordered.reshape(hid, width)

    down_grad = take(0, width)
    gate_grad = take(unit, 0).T
    up_grad = take(2 * unit, 0).T
    layer_output, tokens_grad = call(
        functools.partial(combine_kernel, piece),
        [((block_len, piece), bf16), ((block_len, piece), bf16)],
        50_000_000,
        0,
        weight,
        place,
        place_b,
        place_c,
        back,
    )
    return layer_output, tokens_grad, gate_grad[None], up_grad[None], down_grad[None]


def solution(mesh):
    placed = (
        P("expert", "dp"),
        P("expert", None),
        P("expert", None),
        P("expert", "dp", "etp"),
        P("expert", "dp", "etp"),
        P("expert", "etp", "dp"),
        P("expert", "dp"),
    )
    return jax.shard_map(
        local,
        mesh=mesh,
        in_specs=placed,
        out_specs=(
            P("expert", ("dp", "etp")),
            P("expert", ("dp", "etp")),
            P("expert", "dp", "etp"),
            P("expert", "dp", "etp"),
            P("expert", "etp", "dp"),
        ),
        check_vma=False,
    )
```

```python
import functools

import jax
import jax.numpy as jnp
from jax import lax
from jax.experimental import pallas as pl
from jax.experimental.pallas import tpu as pltpu
from jax.sharding import PartitionSpec as P

LANES = 128
f32 = jnp.float32
bf16 = jnp.bfloat16


def mm(left, right, dims):
    return lax.dot_general(left, right, (dims, ((), ())), preferred_element_type=f32)


def swap(x, axis, groups=None):
    return lax.all_to_all(
        x, axis, split_axis=0, concat_axis=0, tiled=True, axis_index_groups=groups
    )


def iota(shape, axis):
    return lax.broadcasted_iota(jnp.int32, shape, axis)


def call(kernel, outs, flops, n_scalar, *args, far=False, scratch=(), room=16):
    smem = pl.BlockSpec(memory_space=pltpu.SMEM)
    vmem = pl.BlockSpec(memory_space=pltpu.VMEM)
    held = pl.BlockSpec(memory_space=pltpu.HBM) if far else vmem
    outs = [jax.ShapeDtypeStruct(*o) for o in outs]
    moved = sum(a.size * a.dtype.itemsize for a in (*args, *outs))
    return pl.pallas_call(
        kernel,
        out_shape=outs,
        in_specs=[smem] * n_scalar + [held] * (len(args) - n_scalar),
        out_specs=[vmem] * len(outs),
        scratch_shapes=list(scratch),
        compiler_params=pltpu.CompilerParams(vmem_limit_bytes=room * 1024 * 1024),
        cost_estimate=pl.CostEstimate(flops=flops, bytes_accessed=moved, transcendentals=0),
    )(*args)


CAP = 21
PACK = 32
FOLD = PACK - CAP
HEAD = 240


def dispatch_kernel(
    piece,
    col_ref,
    tok_hbm,
    cot_hbm,
    route_hbm,
    cw_hbm,
    send_ref,
    place_ref,
    place_b_ref,
    place_c_ref,
    weight_ref,
    tok_ref,
    cot_ref,
    route_ref,
    cw_ref,
    sems,
):
    pairs = ((route_hbm, route_ref), (cw_hbm, cw_ref), (tok_hbm, tok_ref), (cot_hbm, cot_ref))
    copies = [pltpu.make_async_copy(a, b, sems.at[i]) for i, (a, b) in enumerate(pairs)]
    for copy in copies:
        copy.start()
    copies[0].wait()
    copies[1].wait()
    width = tok_ref.shape[1]
    top_count, block_len = route_ref.shape
    rows = send_ref.shape[0]
    row = iota((rows, block_len), 0)
    owner = lax.shift_right_logical(row, 5)
    inner = row & (PACK - 1)
    hit = jnp.zeros((rows, block_len), f32)
    weight = jnp.zeros((rows, block_len), f32)
    for k in range(top_count):
        hit_k = owner == route_ref[k : k + 1, :]
        hit = jnp.where(hit_k, 1.0, hit)
        weight = jnp.where(hit_k, cw_ref[k : k + 1, :], weight)
    square = (block_len, block_len)
    earlier = jnp.where(iota(square, 0) < iota(square, 1), 1.0, 0.0).astype(bf16)
    before = mm(hit.astype(bf16), earlier, ((1,), (0,)))
    inner_f = inner.astype(f32)
    folded = jnp.where(inner >= CAP, hit, 0.0)
    place = jnp.where((before == inner_f) & (inner < CAP), hit, 0.0)
    place_b = jnp.where(before == inner_f - CAP, folded, 0.0)
    place_c = jnp.where(before == inner_f - (CAP - FOLD), folded, 0.0)
    place_ref[...] = place.astype(bf16)
    place_b_ref[...] = place_b.astype(bf16)
    place_c_ref[...] = place_c.astype(bf16)
    weight_ref[...] = weight * place
    pick_row = iota((width, LANES), 0) - col_ref[0]
    lane = iota((width, LANES), 1)
    pick_x = jnp.where((pick_row == lane) & (lane < piece), 1.0, 0.0).astype(bf16)
    pick_g = jnp.where((pick_row == lane - piece) & (lane >= piece), 1.0, 0.0).astype(bf16)
    rest = (lane & 63) + (LANES - piece)
    pick_r = jnp.where(pick_row == rest, 1.0, 0.0).astype(bf16)
    copies[2].wait()
    copies[3].wait()
    cot = cot_ref[...]
    first = mm(tok_ref[...], pick_x, ((1,), (0,))) + mm(cot, pick_g, ((1,), (0,)))
    last = mm(cot, pick_r, ((1,), (0,))).astype(bf16)
    lanes = iota((rows, LANES), 1)
    scale = jnp.sum(weight * place, axis=1, keepdims=True)
    scale_b = jnp.sum(weight * place_b, axis=1, keepdims=True)
    scale_c = jnp.sum(weight * place_c, axis=1, keepdims=True)
    a = mm(place.astype(bf16), first.astype(bf16), ((1,), (0,)))
    b = mm(place_b.astype(bf16), last, ((1,), (0,)))
    c = mm(place_c.astype(bf16), last, ((1,), (0,)))
    a = jnp.where(lanes < piece, a, a * scale)
    send_ref[...] = (a + jnp.where(lanes < 64, b * scale_b, c * scale_c)).astype(bf16)


def selectors(slots, rows, flip):
    shape, slot_axis = ((rows, slots), 1) if flip else ((slots, rows), 0)
    slot = iota(shape, slot_axis)
    row = iota(shape, 1 - slot_axis)
    base = lax.shift_right_logical(row, 5) * CAP
    inner = row & (PACK - 1)
    at = slot - base
    sel_a = jnp.where((at == inner) & (inner < CAP), 1.0, 0.0).astype(bf16)
    low = at == inner - CAP
    high = (at == inner - (CAP - FOLD)) & (inner < PACK - 1)
    sel_b = jnp.where((low | high) & (inner >= CAP), 1.0, 0.0).astype(bf16)
    return sel_a, sel_b


def is_low(slots, lanes):
    slot = iota((slots, lanes), 0)
    rank = slot - lax.shift_right_logical(slot * 3121, 16) * CAP
    return rank < FOLD


def partials(half_ref, xg, w_ref, part_ref):
    chunks = part_ref.shape[0]
    for j in range(0, chunks, 2):
        at = half_ref[0] + 2 * j
        w = jnp.concatenate([w_ref[at], w_ref[at + 2]], axis=0)
        got = mm(xg, w, ((1,), (1,))).astype(bf16)
        part_ref[j] = got[:, :LANES]
        part_ref[j + 1] = got[:, LANES:]


def first_kernel(piece, half_ref, pack_ref, w_ref, part_ref, xg_ref):
    n_etp, rows, _ = pack_ref.shape
    slots = part_ref.shape[1]
    sel_a, sel_b = selectors(slots, rows, False)
    packed = jnp.concatenate([pack_ref[i] for i in range(n_etp)], axis=1)
    a = mm(sel_a, packed, ((1,), (0,)))
    b = mm(sel_b, packed, ((1,), (0,)))
    low = is_low(slots, 64)
    parts_x, parts_g = [], []
    for i in range(n_etp):
        at = LANES * i
        parts_x.append(a[:, at : at + piece])
        parts_g.append(a[:, at + piece : at + LANES])
        parts_g.append(jnp.where(low, b[:, at : at + 64], b[:, at + 64 : at + LANES]))
    xg = jnp.concatenate(parts_x + parts_g, axis=1).astype(bf16)
    xg_ref[...] = xg
    partials(half_ref, xg, w_ref, part_ref)


def second_kernel(half_ref, xg_ref, w_ref, part_ref):
    partials(half_ref, xg_ref[...], w_ref, part_ref)


def act_kernel(unit, sum_ref, act_ref):
    total = sum_ref[0].astype(f32)
    for j in range(1, sum_ref.shape[0]):
        total = total + sum_ref[j].astype(f32)
    keep = iota(total.shape, 1) < unit
    gate = jnp.where(keep, total, 0.0)
    up = jnp.where(keep, pltpu.roll(total, LANES - unit, 1), 0.0)
    d_hidden = jnp.where(keep, pltpu.roll(total, LANES - 2 * unit, 1), 0.0)
    sig = jax.nn.sigmoid(gate)
    hidden = gate * sig * up
    d_gate = d_hidden * up * sig * (1.0 + gate * (1.0 - sig))
    d_up = d_hidden * gate * sig
    act_ref[...] = (
        hidden + pltpu.roll(d_gate, unit, 1) + pltpu.roll(d_up, 2 * unit, 1)
    ).astype(bf16)


def back_kernel(piece, head_ref, tail_ref, w_ref, pack_ref):
    chunks, slots = head_ref.shape[0], head_ref.shape[1] + tail_ref.shape[1]
    n_etp, rows, _ = pack_ref.shape
    width = w_ref.shape[2] // 2
    act = jnp.concatenate(
        [
            jnp.concatenate([ref[j] for j in range(chunks)], axis=1)
            for ref in (head_ref, tail_ref)
        ],
        axis=0,
    )
    total = mm(act, w_ref[...].reshape(chunks * LANES, 2 * width), ((1,), (0,)))
    total = total.astype(bf16).astype(f32)
    sel_a, sel_b = selectors(slots, rows, True)
    low = is_low(slots, 64)
    parts_a, parts_b = [], []
    for i in range(n_etp):
        parts_a.append(total[:, piece * i : piece * (i + 1)])
        at = width + piece * i
        parts_a.append(total[:, at : at + LANES - piece])
        tail = total[:, at + LANES - piece : at + piece]
        parts_b.append(jnp.where(low, tail, 0.0))
        parts_b.append(jnp.where(low, 0.0, tail))
    a = jnp.concatenate(parts_a, axis=1).astype(bf16)
    b = jnp.concatenate(parts_b, axis=1).astype(bf16)
    packed = (mm(sel_a, a, ((1,), (0,))) + mm(sel_b, b, ((1,), (0,)))).astype(bf16)
    for i in range(n_etp):
        pack_ref[i] = packed[:, LANES * i : LANES * (i + 1)]


def combine_kernel(
    piece, weight_ref, place_ref, place_b_ref, place_c_ref, back_ref, out_ref, grad_ref
):
    back = back_ref[...]
    rest = weight_ref[...]
    total = None
    for _ in range(3):
        high = rest.astype(bf16)
        rest = rest - high.astype(f32)
        term = mm(high, back, ((0,), (0,)))
        total = term if total is None else total + term
    out_ref[...] = total[:, :piece].astype(bf16)
    a = mm(place_ref[...], back, ((0,), (0,)))
    b = mm(place_b_ref[...], back, ((0,), (0,)))
    c = mm(place_c_ref[...], back, ((0,), (0,)))
    grad_ref[...] = jnp.concatenate(
        [a[:, piece:LANES], b[:, :64] + c[:, 64:]], axis=1
    ).astype(bf16)


def local(tokens, routes, combine_weights, gate_weight, up_weight, down_weight, out_cotangent):
    block_len, top_count = routes.shape
    n_exp = lax.axis_size("expert")
    n_etp = lax.axis_size("etp")
    n_dp = lax.axis_size("dp")
    n_y = n_dp // 2
    width = tokens.shape[1]
    piece = width // n_etp
    hid = gate_weight.shape[2]
    unit = hid // n_dp
    slots = n_exp * CAP
    rows = n_exp * PACK
    same_core = [[2 * y + c for y in range(n_y)] for c in range(2)]
    other_core = [(i, i ^ 1) for i in range(n_dp)]
    core = lax.bitwise_and(lax.axis_index("dp"), 1)
    mine, theirs = core[None], (1 - core)[None]
    col = lax.axis_index("etp") * piece

    send, place, place_b, place_c, weight = call(
        functools.partial(dispatch_kernel, piece),
        [
            ((rows, LANES), bf16),
            ((rows, block_len), bf16),
            ((rows, block_len), bf16),
            ((rows, block_len), bf16),
            ((rows, block_len), f32),
        ],
        60_000_000,
        1,
        col[None],
        tokens,
        out_cotangent,
        routes.T,
        combine_weights.T,
        far=True,
        room=60,
        scratch=[
            pltpu.VMEM(tokens.shape, bf16),
            pltpu.VMEM(out_cotangent.shape, bf16),
            pltpu.VMEM((top_count, block_len), jnp.int32),
            pltpu.VMEM((top_count, block_len), f32),
            pltpu.SemaphoreType.DMA((4,)),
        ],
    )
    send, gate_weight, up_weight, down_weight = lax.optimization_barrier(
        (send, gate_weight, up_weight, down_weight)
    )
    w_gate = gate_weight[0].T.reshape(n_dp, unit, width)
    w_up = up_weight[0].T.reshape(n_dp, unit, width)
    w_down = down_weight[0].reshape(n_dp, unit, width)
    spare = LANES - 3 * unit

    def zeros(n):
        return jnp.zeros((n_dp, n, width), bf16)

    w_front = jnp.concatenate(
        [
            jnp.concatenate([w_gate, w_up, zeros(unit + spare)], axis=1),
            jnp.concatenate([zeros(2 * unit), w_down, zeros(spare)], axis=1),
        ],
        axis=2,
    )

    got = swap(send.reshape(n_exp, PACK, LANES), "expert").reshape(1, rows, LANES)
    packs = swap(jnp.broadcast_to(got, (n_etp, rows, LANES)), "etp")

    half_flops = 2 * slots * 2 * width * n_y * LANES
    part_shape = ((n_y, slots, LANES), bf16)
    part_theirs, xg = call(
        functools.partial(first_kernel, piece),
        [part_shape, ((slots, 2 * width), bf16)],
        2 * half_flops,
        1,
        theirs,
        packs,
        w_front,
    )
    part_theirs, w_gate, w_up, w_down = lax.optimization_barrier(
        (part_theirs, w_gate, w_up, w_down)
    )
    w_back = jnp.concatenate(
        [
            jnp.concatenate([w_down, zeros(2 * unit + spare)], axis=1),
            jnp.concatenate([zeros(unit), w_gate, w_up, zeros(spare)], axis=1),
        ],
        axis=2,
    )
    arrived = lax.ppermute(part_theirs, "dp", other_core)
    (part_mine,) = call(second_kernel, [part_shape], half_flops, 1, mine, xg, w_front)
    chip = (part_mine.astype(f32) + arrived.astype(f32)).astype(bf16)
    sums, w_back = lax.optimization_barrier((swap(chip, "dp", same_core), w_back))
    (act,) = call(
        functools.partial(act_kernel, unit),
        [((slots, LANES), bf16)],
        10_000_000,
        0,
        sums,
    )
    tail = jnp.broadcast_to(act[HEAD:], (n_dp, slots - HEAD, LANES))
    tail = swap(tail, "dp")
    head = lax.all_gather(act[:HEAD], "dp", axis=0)
    (out,) = call(
        functools.partial(back_kernel, piece),
        [((n_etp, rows, LANES), bf16)],
        4 * half_flops,
        0,
        head,
        tail,
        w_back,
    )
    out = jnp.sum(swap(out, "etp").astype(f32), axis=0).astype(bf16)
    back = swap(out.reshape(n_exp, PACK, LANES), "expert").reshape(rows, LANES)

    full = jnp.concatenate([head, tail], axis=1)
    grads = mm(full, xg, ((1,), (0,))).astype(bf16)

    def take(start, at):
        return grads[:, start : start + unit, at : at + width].reshape(hid, width)

    down_grad = take(0, width)
    gate_grad = take(unit, 0).T
    up_grad = take(2 * unit, 0).T
    layer_output, tokens_grad = call(
        functools.partial(combine_kernel, piece),
        [((block_len, piece), bf16), ((block_len, piece), bf16)],
        50_000_000,
        0,
        weight,
        place,
        place_b,
        place_c,
        back,
    )
    return layer_output, tokens_grad, gate_grad[None], up_grad[None], down_grad[None]


def solution(mesh):
    placed = (
        P("expert", "dp"),
        P("expert", None),
        P("expert", None),
        P("expert", "dp", "etp"),
        P("expert", "dp", "etp"),
        P("expert", "etp", "dp"),
        P("expert", "dp"),
    )
    return jax.shard_map(
        local,
        mesh=mesh,
        in_specs=placed,
        out_specs=(
            P("expert", ("dp", "etp")),
            P("expert", ("dp", "etp")),
            P("expert", "dp", "etp"),
            P("expert", "dp", "etp"),
            P("expert", "etp", "dp"),
        ),
        check_vma=False,
    )
```

```python
import functools

import jax
import jax.numpy as jnp
from jax import lax
from jax.experimental import pallas as pl
from jax.experimental.pallas import tpu as pltpu
from jax.sharding import PartitionSpec as P

LANES = 128
f32 = jnp.float32
bf16 = jnp.bfloat16


def mm(left, right, dims):
    return lax.dot_general(left, right, (dims, ((), ())), preferred_element_type=f32)


def swap(x, axis, groups=None):
    return lax.all_to_all(
        x, axis, split_axis=0, concat_axis=0, tiled=True, axis_index_groups=groups
    )


def iota(shape, axis):
    return lax.broadcasted_iota(jnp.int32, shape, axis)


def call(kernel, outs, flops, n_scalar, *args, far=False, scratch=(), room=16):
    smem = pl.BlockSpec(memory_space=pltpu.SMEM)
    vmem = pl.BlockSpec(memory_space=pltpu.VMEM)
    held = pl.BlockSpec(memory_space=pltpu.HBM) if far else vmem
    outs = [jax.ShapeDtypeStruct(*o) for o in outs]
    moved = sum(a.size * a.dtype.itemsize for a in (*args, *outs))
    return pl.pallas_call(
        kernel,
        out_shape=outs,
        in_specs=[smem] * n_scalar + [held] * (len(args) - n_scalar),
        out_specs=[vmem] * len(outs),
        scratch_shapes=list(scratch),
        compiler_params=pltpu.CompilerParams(vmem_limit_bytes=room * 1024 * 1024),
        cost_estimate=pl.CostEstimate(flops=flops, bytes_accessed=moved, transcendentals=0),
    )(*args)


CAP = 21
PACK = 32
FOLD = PACK - CAP
HEAD = 240


def dispatch_kernel(
    piece,
    col_ref,
    tok_hbm,
    cot_hbm,
    route_hbm,
    cw_hbm,
    send_ref,
    place_ref,
    place_b_ref,
    place_c_ref,
    weight_ref,
    tok_ref,
    cot_ref,
    route_ref,
    cw_ref,
    sems,
):
    pairs = ((route_hbm, route_ref), (cw_hbm, cw_ref), (tok_hbm, tok_ref), (cot_hbm, cot_ref))
    copies = [pltpu.make_async_copy(a, b, sems.at[i]) for i, (a, b) in enumerate(pairs)]
    for copy in copies:
        copy.start()
    copies[0].wait()
    copies[1].wait()
    width = tok_ref.shape[1]
    top_count, block_len = route_ref.shape
    rows = send_ref.shape[0]
    row = iota((rows, block_len), 0)
    owner = lax.shift_right_logical(row, 5)
    inner = row & (PACK - 1)
    hit = jnp.zeros((rows, block_len), f32)
    weight = jnp.zeros((rows, block_len), f32)
    for k in range(top_count):
        hit_k = owner == route_ref[k : k + 1, :]
        hit = jnp.where(hit_k, 1.0, hit)
        weight = jnp.where(hit_k, cw_ref[k : k + 1, :], weight)
    square = (block_len, block_len)
    earlier = jnp.where(iota(square, 0) < iota(square, 1), 1.0, 0.0).astype(bf16)
    before = mm(hit.astype(bf16), earlier, ((1,), (0,)))
    inner_f = inner.astype(f32)
    folded = jnp.where(inner >= CAP, hit, 0.0)
    place = jnp.where((before == inner_f) & (inner < CAP), hit, 0.0)
    place_b = jnp.where(before == inner_f - CAP, folded, 0.0)
    place_c = jnp.where(before == inner_f - (CAP - FOLD), folded, 0.0)
    place_ref[...] = place.astype(bf16)
    place_b_ref[...] = place_b.astype(bf16)
    place_c_ref[...] = place_c.astype(bf16)
    weight_ref[...] = weight * place
    pick_row = iota((width, LANES), 0) - col_ref[0]
    lane = iota((width, LANES), 1)
    pick_x = jnp.where((pick_row == lane) & (lane < piece), 1.0, 0.0).astype(bf16)
    pick_g = jnp.where((pick_row == lane - piece) & (lane >= piece), 1.0, 0.0).astype(bf16)
    rest = (lane & 63) + (LANES - piece)
    pick_r = jnp.where(pick_row == rest, 1.0, 0.0).astype(bf16)
    copies[2].wait()
    copies[3].wait()
    cot = cot_ref[...]
    first = mm(tok_ref[...], pick_x, ((1,), (0,))) + mm(cot, pick_g, ((1,), (0,)))
    last = mm(cot, pick_r, ((1,), (0,))).astype(bf16)
    lanes = iota((rows, LANES), 1)
    scale = jnp.sum(weight * place, axis=1, keepdims=True)
    scale_b = jnp.sum(weight * place_b, axis=1, keepdims=True)
    scale_c = jnp.sum(weight * place_c, axis=1, keepdims=True)
    a = mm(place.astype(bf16), first.astype(bf16), ((1,), (0,)))
    b = mm(place_b.astype(bf16), last, ((1,), (0,)))
    c = mm(place_c.astype(bf16), last, ((1,), (0,)))
    a = jnp.where(lanes < piece, a, a * scale)
    send_ref[...] = (a + jnp.where(lanes < 64, b * scale_b, c * scale_c)).astype(bf16)


def selectors(slots, rows, flip):
    shape, slot_axis = ((rows, slots), 1) if flip else ((slots, rows), 0)
    slot = iota(shape, slot_axis)
    row = iota(shape, 1 - slot_axis)
    base = lax.shift_right_logical(row, 5) * CAP
    inner = row & (PACK - 1)
    at = slot - base
    sel_a = jnp.where((at == inner) & (inner < CAP), 1.0, 0.0).astype(bf16)
    low = at == inner - CAP
    high = (at == inner - (CAP - FOLD)) & (inner < PACK - 1)
    sel_b = jnp.where((low | high) & (inner >= CAP), 1.0, 0.0).astype(bf16)
    return sel_a, sel_b


def is_low(slots, lanes):
    slot = iota((slots, lanes), 0)
    rank = slot - lax.shift_right_logical(slot * 3121, 16) * CAP
    return rank < FOLD


def partials(half_ref, xg, w_ref, part_ref):
    chunks = part_ref.shape[0]
    for j in range(0, chunks, 2):
        at = half_ref[0] + 2 * j
        w = jnp.concatenate([w_ref[at], w_ref[at + 2]], axis=0)
        got = mm(xg, w, ((1,), (1,))).astype(bf16)
        part_ref[j] = got[:, :LANES]
        part_ref[j + 1] = got[:, LANES:]


def first_kernel(piece, half_ref, pack_ref, w_ref, part_ref, xg_ref):
    n_etp, rows, _ = pack_ref.shape
    slots = part_ref.shape[1]
    sel_a, sel_b = selectors(slots, rows, False)
    packed = jnp.concatenate([pack_ref[i] for i in range(n_etp)], axis=1)
    a = mm(sel_a, packed, ((1,), (0,)))
    b = mm(sel_b, packed, ((1,), (0,)))
    low = is_low(slots, 64)
    parts_x, parts_g = [], []
    for i in range(n_etp):
        at = LANES * i
        parts_x.append(a[:, at : at + piece])
        parts_g.append(a[:, at + piece : at + LANES])
        parts_g.append(jnp.where(low, b[:, at : at + 64], b[:, at + 64 : at + LANES]))
    xg = jnp.concatenate(parts_x + parts_g, axis=1).astype(bf16)
    xg_ref[...] = xg
    partials(half_ref, xg, w_ref, part_ref)


def second_kernel(half_ref, xg_ref, w_ref, part_ref):
    partials(half_ref, xg_ref[...], w_ref, part_ref)


def act_kernel(unit, sum_ref, head_ref, tail_ref):
    total = sum_ref[0].astype(f32)
    for j in range(1, sum_ref.shape[0]):
        total = total + sum_ref[j].astype(f32)
    keep = iota(total.shape, 1) < unit
    gate = jnp.where(keep, total, 0.0)
    up = jnp.where(keep, pltpu.roll(total, LANES - unit, 1), 0.0)
    d_hidden = jnp.where(keep, pltpu.roll(total, LANES - 2 * unit, 1), 0.0)
    sig = jax.nn.sigmoid(gate)
    hidden = gate * sig * up
    d_gate = d_hidden * up * sig * (1.0 + gate * (1.0 - sig))
    d_up = d_hidden * gate * sig
    act = d_gate + pltpu.roll(d_up, unit, 1) + pltpu.roll(hidden, 2 * unit, 1)
    act = act.astype(bf16)
    n_head = head_ref.shape[0]
    head_ref[...] = act[:n_head]
    for j in range(tail_ref.shape[0]):
        tail_ref[j] = act[n_head:]


def back_kernel(piece, head_ref, tail_ref, w_ref, pack_ref):
    chunks, slots = head_ref.shape[0], head_ref.shape[1] + tail_ref.shape[1]
    n_etp, rows, _ = pack_ref.shape
    width = w_ref.shape[2] // 2
    act = jnp.concatenate(
        [
            jnp.concatenate([ref[j] for j in range(chunks)], axis=1)
            for ref in (head_ref, tail_ref)
        ],
        axis=0,
    )
    total = mm(act, w_ref[...].reshape(chunks * LANES, 2 * width), ((1,), (0,)))
    total = total.astype(bf16).astype(f32)
    sel_a, sel_b = selectors(slots, rows, True)
    low = is_low(slots, 64)
    parts_a, parts_b = [], []
    for i in range(n_etp):
        at = piece * i
        parts_a.append(total[:, width + at : width + at + piece])
        parts_a.append(total[:, at : at + LANES - piece])
        tail = total[:, at + LANES - piece : at + piece]
        parts_b.append(jnp.where(low, tail, 0.0))
        parts_b.append(jnp.where(low, 0.0, tail))
    a = jnp.concatenate(parts_a, axis=1).astype(bf16)
    b = jnp.concatenate(parts_b, axis=1).astype(bf16)
    packed = (mm(sel_a, a, ((1,), (0,))) + mm(sel_b, b, ((1,), (0,)))).astype(bf16)
    for i in range(n_etp):
        pack_ref[i] = packed[:, LANES * i : LANES * (i + 1)]


def combine_kernel(
    piece, weight_ref, place_ref, place_b_ref, place_c_ref, back_ref, out_ref, grad_ref
):
    back = back_ref[...]
    rest = weight_ref[...]
    total = None
    for _ in range(3):
        high = rest.astype(bf16)
        rest = rest - high.astype(f32)
        term = mm(high, back, ((0,), (0,)))
        total = term if total is None else total + term
    out_ref[...] = total[:, :piece].astype(bf16)
    a = mm(place_ref[...], back, ((0,), (0,)))
    b = mm(place_b_ref[...], back, ((0,), (0,)))
    c = mm(place_c_ref[...], back, ((0,), (0,)))
    grad_ref[...] = jnp.concatenate(
        [a[:, piece:LANES], b[:, :64] + c[:, 64:]], axis=1
    ).astype(bf16)


def local(tokens, routes, combine_weights, gate_weight, up_weight, down_weight, out_cotangent):
    block_len, top_count = routes.shape
    n_exp = lax.axis_size("expert")
    n_etp = lax.axis_size("etp")
    n_dp = lax.axis_size("dp")
    n_y = n_dp // 2
    width = tokens.shape[1]
    piece = width // n_etp
    hid = gate_weight.shape[2]
    unit = hid // n_dp
    slots = n_exp * CAP
    rows = n_exp * PACK
    same_core = [[2 * y + c for y in range(n_y)] for c in range(2)]
    other_core = [(i, i ^ 1) for i in range(n_dp)]
    core = lax.bitwise_and(lax.axis_index("dp"), 1)
    mine, theirs = core[None], (1 - core)[None]
    col = lax.axis_index("etp") * piece

    send, place, place_b, place_c, weight = call(
        functools.partial(dispatch_kernel, piece),
        [
            ((rows, LANES), bf16),
            ((rows, block_len), bf16),
            ((rows, block_len), bf16),
            ((rows, block_len), bf16),
            ((rows, block_len), f32),
        ],
        60_000_000,
        1,
        col[None],
        tokens,
        out_cotangent,
        routes.T,
        combine_weights.T,
        far=True,
        room=60,
        scratch=[
            pltpu.VMEM(tokens.shape, bf16),
            pltpu.VMEM(out_cotangent.shape, bf16),
            pltpu.VMEM((top_count, block_len), jnp.int32),
            pltpu.VMEM((top_count, block_len), f32),
            pltpu.SemaphoreType.DMA((4,)),
        ],
    )
    send, gate_weight, up_weight, down_weight = lax.optimization_barrier(
        (send, gate_weight, up_weight, down_weight)
    )
    w_gate = gate_weight[0].T.reshape(n_dp, unit, width)
    w_up = up_weight[0].T.reshape(n_dp, unit, width)
    w_down = down_weight[0].reshape(n_dp, unit, width)
    spare = LANES - 3 * unit

    def zeros(n):
        return jnp.zeros((n_dp, n, width), bf16)

    w_front = jnp.concatenate(
        [
            jnp.concatenate([w_gate, w_up, zeros(unit + spare)], axis=1),
            jnp.concatenate([zeros(2 * unit), w_down, zeros(spare)], axis=1),
        ],
        axis=2,
    )

    got = swap(send.reshape(n_exp, PACK, LANES), "expert").reshape(1, rows, LANES)
    got, w_front = lax.optimization_barrier((got, w_front))
    packs = swap(jnp.broadcast_to(got, (n_etp, rows, LANES)), "etp")

    half_flops = 2 * slots * 2 * width * n_y * LANES
    part_shape = ((n_y, slots, LANES), bf16)
    part_theirs, xg = call(
        functools.partial(first_kernel, piece),
        [part_shape, ((slots, 2 * width), bf16)],
        2 * half_flops,
        1,
        theirs,
        packs,
        w_front,
    )
    arrived = lax.ppermute(part_theirs, "dp", other_core)
    (part_mine,) = call(second_kernel, [part_shape], half_flops, 1, mine, xg, w_front)
    chip = (part_mine.astype(f32) + arrived.astype(f32)).astype(bf16)
    head, tail = call(
        functools.partial(act_kernel, unit),
        [((HEAD, LANES), bf16), ((n_dp, slots - HEAD, LANES), bf16)],
        10_000_000,
        0,
        swap(chip, "dp", same_core),
    )
    tail = swap(tail, "dp")
    head = lax.all_gather(head, "dp", axis=0)
    (out,) = call(
        functools.partial(back_kernel, piece),
        [((n_etp, rows, LANES), bf16)],
        4 * half_flops,
        0,
        head,
        tail,
        w_front,
    )
    out = jnp.sum(swap(out, "etp").astype(f32), axis=0).astype(bf16)
    back = swap(out.reshape(n_exp, PACK, LANES), "expert").reshape(rows, LANES)

    full = jnp.concatenate([head, tail], axis=1)
    grads = mm(full, xg, ((1,), (0,))).astype(bf16)

    def take(start, at):
        return grads[:, start : start + unit, at : at + width].reshape(hid, width)

    gate_grad = take(0, 0).T
    up_grad = take(unit, 0).T
    down_grad = take(2 * unit, width)
    layer_output, tokens_grad = call(
        functools.partial(combine_kernel, piece),
        [((block_len, piece), bf16), ((block_len, piece), bf16)],
        50_000_000,
        0,
        weight,
        place,
        place_b,
        place_c,
        back,
    )
    return layer_output, tokens_grad, gate_grad[None], up_grad[None], down_grad[None]


def solution(mesh):
    placed = (
        P("expert", "dp"),
        P("expert", None),
        P("expert", None),
        P("expert", "dp", "etp"),
        P("expert", "dp", "etp"),
        P("expert", "etp", "dp"),
        P("expert", "dp"),
    )
    return jax.shard_map(
        local,
        mesh=mesh,
        in_specs=placed,
        out_specs=(
            P("expert", ("dp", "etp")),
            P("expert", ("dp", "etp")),
            P("expert", "dp", "etp"),
            P("expert", "dp", "etp"),
            P("expert", "etp", "dp"),
        ),
        check_vma=False,
    )
```

```python
import functools

import jax
import jax.numpy as jnp
from jax import lax
from jax.experimental import pallas as pl
from jax.experimental.pallas import tpu as pltpu
from jax.sharding import PartitionSpec as P

LANES = 128
f32 = jnp.float32
bf16 = jnp.bfloat16


def mm(left, right, dims):
    return lax.dot_general(left, right, (dims, ((), ())), preferred_element_type=f32)


def swap(x, axis, groups=None):
    return lax.all_to_all(
        x, axis, split_axis=0, concat_axis=0, tiled=True, axis_index_groups=groups
    )


def iota(shape, axis):
    return lax.broadcasted_iota(jnp.int32, shape, axis)


def call(kernel, outs, flops, n_scalar, *args, far=False, scratch=(), room=16):
    smem = pl.BlockSpec(memory_space=pltpu.SMEM)
    vmem = pl.BlockSpec(memory_space=pltpu.VMEM)
    held = pl.BlockSpec(memory_space=pltpu.HBM) if far else vmem
    outs = [jax.ShapeDtypeStruct(*o) for o in outs]
    moved = sum(a.size * a.dtype.itemsize for a in (*args, *outs))
    return pl.pallas_call(
        kernel,
        out_shape=outs,
        in_specs=[smem] * n_scalar + [held] * (len(args) - n_scalar),
        out_specs=[vmem] * len(outs),
        scratch_shapes=list(scratch),
        compiler_params=pltpu.CompilerParams(vmem_limit_bytes=room * 1024 * 1024),
        cost_estimate=pl.CostEstimate(flops=flops, bytes_accessed=moved, transcendentals=0),
    )(*args)


CAP = 21
PACK = 32
FOLD = PACK - CAP
HEAD = 240


def dispatch_kernel(
    piece,
    col_ref,
    tok_hbm,
    cot_hbm,
    route_hbm,
    cw_hbm,
    send_ref,
    place_ref,
    place_b_ref,
    place_c_ref,
    weight_ref,
    tok_ref,
    cot_ref,
    route_ref,
    cw_ref,
    sems,
):
    pairs = ((route_hbm, route_ref), (cw_hbm, cw_ref), (tok_hbm, tok_ref), (cot_hbm, cot_ref))
    copies = [pltpu.make_async_copy(a, b, sems.at[i]) for i, (a, b) in enumerate(pairs)]
    for copy in copies:
        copy.start()
    copies[0].wait()
    copies[1].wait()
    width = tok_ref.shape[1]
    top_count, block_len = route_ref.shape
    rows = send_ref.shape[0]
    row = iota((rows, block_len), 0)
    owner = lax.shift_right_logical(row, 5)
    inner = row & (PACK - 1)
    hit = jnp.zeros((rows, block_len), f32)
    weight = jnp.zeros((rows, block_len), f32)
    for k in range(top_count):
        hit_k = owner == route_ref[k : k + 1, :]
        hit = jnp.where(hit_k, 1.0, hit)
        weight = jnp.where(hit_k, cw_ref[k : k + 1, :], weight)
    square = (block_len, block_len)
    earlier = jnp.where(iota(square, 0) < iota(square, 1), 1.0, 0.0).astype(bf16)
    before = mm(hit.astype(bf16), earlier, ((1,), (0,)))
    inner_f = inner.astype(f32)
    folded = jnp.where(inner >= CAP, hit, 0.0)
    place = jnp.where((before == inner_f) & (inner < CAP), hit, 0.0)
    place_b = jnp.where(before == inner_f - CAP, folded, 0.0)
    place_c = jnp.where(before == inner_f - (CAP - FOLD), folded, 0.0)
    place_ref[...] = place.astype(bf16)
    place_b_ref[...] = place_b.astype(bf16)
    place_c_ref[...] = place_c.astype(bf16)
    weight_ref[...] = weight * place
    pick_row = iota((width, LANES), 0) - col_ref[0]
    lane = iota((width, LANES), 1)
    pick_x = jnp.where((pick_row == lane) & (lane < piece), 1.0, 0.0).astype(bf16)
    pick_g = jnp.where((pick_row == lane - piece) & (lane >= piece), 1.0, 0.0).astype(bf16)
    rest = (lane & 63) + (LANES - piece)
    pick_r = jnp.where(pick_row == rest, 1.0, 0.0).astype(bf16)
    copies[2].wait()
    copies[3].wait()
    cot = cot_ref[...]
    first = mm(tok_ref[...], pick_x, ((1,), (0,))) + mm(cot, pick_g, ((1,), (0,)))
    last = mm(cot, pick_r, ((1,), (0,))).astype(bf16)
    lanes = iota((rows, LANES), 1)
    scale = jnp.sum(weight * place, axis=1, keepdims=True)
    scale_b = jnp.sum(weight * place_b, axis=1, keepdims=True)
    scale_c = jnp.sum(weight * place_c, axis=1, keepdims=True)
    a = mm(place.astype(bf16), first.astype(bf16), ((1,), (0,)))
    b = mm(place_b.astype(bf16), last, ((1,), (0,)))
    c = mm(place_c.astype(bf16), last, ((1,), (0,)))
    a = jnp.where(lanes < piece, a, a * scale)
    send_ref[...] = (a + jnp.where(lanes < 64, b * scale_b, c * scale_c)).astype(bf16)


def selectors(slots, rows, flip):
    shape, slot_axis = ((rows, slots), 1) if flip else ((slots, rows), 0)
    slot = iota(shape, slot_axis)
    row = iota(shape, 1 - slot_axis)
    base = lax.shift_right_logical(row, 5) * CAP
    inner = row & (PACK - 1)
    at = slot - base
    sel_a = jnp.where((at == inner) & (inner < CAP), 1.0, 0.0).astype(bf16)
    low = at == inner - CAP
    high = (at == inner - (CAP - FOLD)) & (inner < PACK - 1)
    sel_b = jnp.where((low | high) & (inner >= CAP), 1.0, 0.0).astype(bf16)
    return sel_a, sel_b


def is_low(slots, lanes):
    slot = iota((slots, lanes), 0)
    rank = slot - lax.shift_right_logical(slot * 3121, 16) * CAP
    return rank < FOLD


def partials(split, half_ref, xg, w_ref, part_ref):
    chunks = part_ref.shape[0]
    width = w_ref.shape[2]
    from_x = (iota((xg.shape[0], 2 * LANES), 1) & (LANES - 1)) < split
    for j in range(0, chunks, 2):
        at = half_ref[0] + 2 * j
        w = jnp.concatenate([w_ref[at], w_ref[at + 2]], axis=0)
        by_x = mm(xg[:, :width], w, ((1,), (1,)))
        by_g = mm(xg[:, width:], w, ((1,), (1,)))
        got = jnp.where(from_x, by_x, by_g).astype(bf16)
        part_ref[j] = got[:, :LANES]
        part_ref[j + 1] = got[:, LANES:]


def first_kernel(piece, split, half_ref, pack_ref, w_ref, part_ref, xg_ref):
    n_etp, rows, _ = pack_ref.shape
    slots = part_ref.shape[1]
    sel_a, sel_b = selectors(slots, rows, False)
    packed = jnp.concatenate([pack_ref[i] for i in range(n_etp)], axis=1)
    a = mm(sel_a, packed, ((1,), (0,)))
    b = mm(sel_b, packed, ((1,), (0,)))
    low = is_low(slots, 64)
    parts_x, parts_g = [], []
    for i in range(n_etp):
        at = LANES * i
        parts_x.append(a[:, at : at + piece])
        parts_g.append(a[:, at + piece : at + LANES])
        parts_g.append(jnp.where(low, b[:, at : at + 64], b[:, at + 64 : at + LANES]))
    xg = jnp.concatenate(parts_x + parts_g, axis=1).astype(bf16)
    xg_ref[...] = xg
    partials(split, half_ref, xg, w_ref, part_ref)


def second_kernel(split, half_ref, xg_ref, w_ref, part_ref):
    partials(split, half_ref, xg_ref[...], w_ref, part_ref)


def act_kernel(unit, sum_ref, head_ref, tail_ref):
    total = sum_ref[0].astype(f32)
    for j in range(1, sum_ref.shape[0]):
        total = total + sum_ref[j].astype(f32)
    keep = iota(total.shape, 1) < unit
    gate = jnp.where(keep, total, 0.0)
    up = jnp.where(keep, pltpu.roll(total, LANES - unit, 1), 0.0)
    d_hidden = jnp.where(keep, pltpu.roll(total, LANES - 2 * unit, 1), 0.0)
    sig = jax.nn.sigmoid(gate)
    hidden = gate * sig * up
    d_gate = d_hidden * up * sig * (1.0 + gate * (1.0 - sig))
    d_up = d_hidden * gate * sig
    act = d_gate + pltpu.roll(d_up, unit, 1) + pltpu.roll(hidden, 2 * unit, 1)
    act = act.astype(bf16)
    n_head = head_ref.shape[0]
    head_ref[...] = act[:n_head]
    for j in range(tail_ref.shape[0]):
        tail_ref[j] = act[n_head:]


def back_kernel(piece, split, head_ref, tail_ref, w_ref, pack_ref):
    chunks, slots = head_ref.shape[0], head_ref.shape[1] + tail_ref.shape[1]
    n_etp, rows, _ = pack_ref.shape
    width = w_ref.shape[2]
    w = w_ref[...].reshape(chunks * LANES, width)
    first = iota((1, LANES), 1) < split

    def product(keep):
        keep = jnp.where(keep, 1.0, 0.0).astype(bf16)
        act = jnp.concatenate(
            [
                jnp.concatenate([ref[j] * keep for j in range(chunks)], axis=1)
                for ref in (head_ref, tail_ref)
            ],
            axis=0,
        )
        return mm(act, w, ((1,), (0,))).astype(bf16).astype(f32)

    dx = product(first)
    y = product(jnp.logical_not(first))
    sel_a, sel_b = selectors(slots, rows, True)
    low = is_low(slots, 64)
    parts_a, parts_b = [], []
    for i in range(n_etp):
        at = piece * i
        parts_a.append(y[:, at : at + piece])
        parts_a.append(dx[:, at : at + LANES - piece])
        tail = dx[:, at + LANES - piece : at + piece]
        parts_b.append(jnp.where(low, tail, 0.0))
        parts_b.append(jnp.where(low, 0.0, tail))
    a = jnp.concatenate(parts_a, axis=1).astype(bf16)
    b = jnp.concatenate(parts_b, axis=1).astype(bf16)
    packed = (mm(sel_a, a, ((1,), (0,))) + mm(sel_b, b, ((1,), (0,)))).astype(bf16)
    for i in range(n_etp):
        pack_ref[i] = packed[:, LANES * i : LANES * (i + 1)]


def combine_kernel(
    piece, weight_ref, place_ref, place_b_ref, place_c_ref, back_ref, out_ref, grad_ref
):
    back = back_ref[...]
    rest = weight_ref[...]
    total = None
    for _ in range(3):
        high = rest.astype(bf16)
        rest = rest - high.astype(f32)
        term = mm(high, back, ((0,), (0,)))
        total = term if total is None else total + term
    out_ref[...] = total[:, :piece].astype(bf16)
    a = mm(place_ref[...], back, ((0,), (0,)))
    b = mm(place_b_ref[...], back, ((0,), (0,)))
    c = mm(place_c_ref[...], back, ((0,), (0,)))
    grad_ref[...] = jnp.concatenate(
        [a[:, piece:LANES], b[:, :64] + c[:, 64:]], axis=1
    ).astype(bf16)


def local(tokens, routes, combine_weights, gate_weight, up_weight, down_weight, out_cotangent):
    block_len, top_count = routes.shape
    n_exp = lax.axis_size("expert")
    n_etp = lax.axis_size("etp")
    n_dp = lax.axis_size("dp")
    n_y = n_dp // 2
    width = tokens.shape[1]
    piece = width // n_etp
    hid = gate_weight.shape[2]
    unit = hid // n_dp
    slots = n_exp * CAP
    rows = n_exp * PACK
    same_core = [[2 * y + c for y in range(n_y)] for c in range(2)]
    other_core = [(i, i ^ 1) for i in range(n_dp)]
    core = lax.bitwise_and(lax.axis_index("dp"), 1)
    mine, theirs = core[None], (1 - core)[None]
    col = lax.axis_index("etp") * piece

    send, place, place_b, place_c, weight = call(
        functools.partial(dispatch_kernel, piece),
        [
            ((rows, LANES), bf16),
            ((rows, block_len), bf16),
            ((rows, block_len), bf16),
            ((rows, block_len), bf16),
            ((rows, block_len), f32),
        ],
        60_000_000,
        1,
        col[None],
        tokens,
        out_cotangent,
        routes.T,
        combine_weights.T,
        far=True,
        room=60,
        scratch=[
            pltpu.VMEM(tokens.shape, bf16),
            pltpu.VMEM(out_cotangent.shape, bf16),
            pltpu.VMEM((top_count, block_len), jnp.int32),
            pltpu.VMEM((top_count, block_len), f32),
            pltpu.SemaphoreType.DMA((4,)),
        ],
    )
    send, gate_weight, up_weight, down_weight = lax.optimization_barrier(
        (send, gate_weight, up_weight, down_weight)
    )
    w_gate = gate_weight[0].T.reshape(n_dp, unit, width)
    w_up = up_weight[0].T.reshape(n_dp, unit, width)
    w_down = down_weight[0].reshape(n_dp, unit, width)
    spare = LANES - 3 * unit

    w_front = jnp.concatenate(
        [w_gate, w_up, w_down, jnp.zeros((n_dp, spare, width), bf16)], axis=1
    )

    got = swap(send.reshape(n_exp, PACK, LANES), "expert").reshape(1, rows, LANES)
    got, w_front = lax.optimization_barrier((got, w_front))
    packs = swap(jnp.broadcast_to(got, (n_etp, rows, LANES)), "etp")

    half_flops = 2 * slots * 2 * width * n_y * LANES
    part_shape = ((n_y, slots, LANES), bf16)
    part_theirs, xg = call(
        functools.partial(first_kernel, piece, 2 * unit),
        [part_shape, ((slots, 2 * width), bf16)],
        2 * half_flops,
        1,
        theirs,
        packs,
        w_front,
    )
    arrived = lax.ppermute(part_theirs, "dp", other_core)
    (part_mine,) = call(
        functools.partial(second_kernel, 2 * unit), [part_shape], half_flops, 1, mine, xg, w_front)
    chip = (part_mine.astype(f32) + arrived.astype(f32)).astype(bf16)
    head, tail = call(
        functools.partial(act_kernel, unit),
        [((HEAD, LANES), bf16), ((n_dp, slots - HEAD, LANES), bf16)],
        10_000_000,
        0,
        swap(chip, "dp", same_core),
    )
    tail = swap(tail, "dp")
    head = lax.all_gather(head, "dp", axis=0)
    (out,) = call(
        functools.partial(back_kernel, piece, 2 * unit),
        [((n_etp, rows, LANES), bf16)],
        4 * half_flops,
        0,
        head,
        tail,
        w_front,
    )
    out = jnp.sum(swap(out, "etp").astype(f32), axis=0).astype(bf16)
    back = swap(out.reshape(n_exp, PACK, LANES), "expert").reshape(rows, LANES)

    full = jnp.concatenate([head, tail], axis=1)
    grads = mm(full, xg, ((1,), (0,))).astype(bf16)

    def take(start, at):
        return grads[:, start : start + unit, at : at + width].reshape(hid, width)

    gate_grad = take(0, 0).T
    up_grad = take(unit, 0).T
    down_grad = take(2 * unit, width)
    layer_output, tokens_grad = call(
        functools.partial(combine_kernel, piece),
        [((block_len, piece), bf16), ((block_len, piece), bf16)],
        50_000_000,
        0,
        weight,
        place,
        place_b,
        place_c,
        back,
    )
    return layer_output, tokens_grad, gate_grad[None], up_grad[None], down_grad[None]


def solution(mesh):
    placed = (
        P("expert", "dp"),
        P("expert", None),
        P("expert", None),
        P("expert", "dp", "etp"),
        P("expert", "dp", "etp"),
        P("expert", "etp", "dp"),
        P("expert", "dp"),
    )
    return jax.shard_map(
        local,
        mesh=mesh,
        in_specs=placed,
        out_specs=(
            P("expert", ("dp", "etp")),
            P("expert", ("dp", "etp")),
            P("expert", "dp", "etp"),
            P("expert", "dp", "etp"),
            P("expert", "etp", "dp"),
        ),
        check_vma=False,
    )
```

```python
import functools

import jax
import jax.numpy as jnp
from jax import lax
from jax.experimental import pallas as pl
from jax.experimental.pallas import tpu as pltpu
from jax.sharding import PartitionSpec as P

LANES = 128
f32 = jnp.float32
bf16 = jnp.bfloat16


def mm(left, right, dims):
    return lax.dot_general(left, right, (dims, ((), ())), preferred_element_type=f32)


def swap(x, axis, groups=None):
    return lax.all_to_all(
        x, axis, split_axis=0, concat_axis=0, tiled=True, axis_index_groups=groups
    )


def iota(shape, axis):
    return lax.broadcasted_iota(jnp.int32, shape, axis)


def call(kernel, outs, flops, n_scalar, *args, far=False, scratch=(), room=16):
    smem = pl.BlockSpec(memory_space=pltpu.SMEM)
    vmem = pl.BlockSpec(memory_space=pltpu.VMEM)
    held = pl.BlockSpec(memory_space=pltpu.HBM) if far else vmem
    outs = [jax.ShapeDtypeStruct(*o) for o in outs]
    moved = sum(a.size * a.dtype.itemsize for a in (*args, *outs))
    return pl.pallas_call(
        kernel,
        out_shape=outs,
        in_specs=[smem] * n_scalar + [held] * (len(args) - n_scalar),
        out_specs=[vmem] * len(outs),
        scratch_shapes=list(scratch),
        compiler_params=pltpu.CompilerParams(vmem_limit_bytes=room * 1024 * 1024),
        cost_estimate=pl.CostEstimate(flops=flops, bytes_accessed=moved, transcendentals=0),
    )(*args)


CAP = 21
PACK = 32
FOLD = PACK - CAP
HEAD = 240


def dispatch_kernel(
    piece,
    col_ref,
    tok_hbm,
    cot_hbm,
    route_hbm,
    cw_hbm,
    send_ref,
    place_ref,
    place_b_ref,
    place_c_ref,
    weight_ref,
    tok_ref,
    cot_ref,
    route_ref,
    cw_ref,
    sems,
):
    pairs = ((route_hbm, route_ref), (cw_hbm, cw_ref), (tok_hbm, tok_ref), (cot_hbm, cot_ref))
    copies = [pltpu.make_async_copy(a, b, sems.at[i]) for i, (a, b) in enumerate(pairs)]
    for copy in copies:
        copy.start()
    copies[0].wait()
    copies[1].wait()
    width = tok_ref.shape[1]
    top_count, block_len = route_ref.shape
    rows = send_ref.shape[0]
    row = iota((rows, block_len), 0)
    owner = lax.shift_right_logical(row, 5)
    inner = row & (PACK - 1)
    hit = jnp.zeros((rows, block_len), f32)
    weight = jnp.zeros((rows, block_len), f32)
    for k in range(top_count):
        hit_k = owner == route_ref[k : k + 1, :]
        hit = jnp.where(hit_k, 1.0, hit)
        weight = jnp.where(hit_k, cw_ref[k : k + 1, :], weight)
    square = (block_len, block_len)
    earlier = jnp.where(iota(square, 0) < iota(square, 1), 1.0, 0.0).astype(bf16)
    before = mm(hit.astype(bf16), earlier, ((1,), (0,)))
    inner_f = inner.astype(f32)
    folded = jnp.where(inner >= CAP, hit, 0.0)
    place = jnp.where((before == inner_f) & (inner < CAP), hit, 0.0)
    place_b = jnp.where(before == inner_f - CAP, folded, 0.0)
    place_c = jnp.where(before == inner_f - (CAP - FOLD), folded, 0.0)
    place_ref[...] = place.astype(bf16)
    place_b_ref[...] = place_b.astype(bf16)
    place_c_ref[...] = place_c.astype(bf16)
    weight_ref[...] = weight * place
    pick_row = iota((width, LANES), 0) - col_ref[0]
    lane = iota((width, LANES), 1)
    pick_x = jnp.where((pick_row == lane) & (lane < piece), 1.0, 0.0).astype(bf16)
    pick_g = jnp.where((pick_row == lane - piece) & (lane >= piece), 1.0, 0.0).astype(bf16)
    rest = (lane & 63) + (LANES - piece)
    pick_r = jnp.where(pick_row == rest, 1.0, 0.0).astype(bf16)
    copies[2].wait()
    copies[3].wait()
    cot = cot_ref[...]
    first = mm(tok_ref[...], pick_x, ((1,), (0,))) + mm(cot, pick_g, ((1,), (0,)))
    last = mm(cot, pick_r, ((1,), (0,))).astype(bf16)
    lanes = iota((rows, LANES), 1)
    scale = jnp.sum(weight * place, axis=1, keepdims=True)
    scale_b = jnp.sum(weight * place_b, axis=1, keepdims=True)
    scale_c = jnp.sum(weight * place_c, axis=1, keepdims=True)
    a = mm(place.astype(bf16), first.astype(bf16), ((1,), (0,)))
    b = mm(place_b.astype(bf16), last, ((1,), (0,)))
    c = mm(place_c.astype(bf16), last, ((1,), (0,)))
    a = jnp.where(lanes < piece, a, a * scale)
    send_ref[...] = (a + jnp.where(lanes < 64, b * scale_b, c * scale_c)).astype(bf16)


def selectors(slots, rows, flip):
    shape, slot_axis = ((rows, slots), 1) if flip else ((slots, rows), 0)
    slot = iota(shape, slot_axis)
    row = iota(shape, 1 - slot_axis)
    base = lax.shift_right_logical(row, 5) * CAP
    inner = row & (PACK - 1)
    at = slot - base
    sel_a = jnp.where((at == inner) & (inner < CAP), 1.0, 0.0).astype(bf16)
    low = at == inner - CAP
    high = (at == inner - (CAP - FOLD)) & (inner < PACK - 1)
    sel_b = jnp.where((low | high) & (inner >= CAP), 1.0, 0.0).astype(bf16)
    return sel_a, sel_b


def is_low(slots, lanes):
    slot = iota((slots, lanes), 0)
    rank = slot - lax.shift_right_logical(slot * 3121, 16) * CAP
    return rank < FOLD


def partials(split, half_ref, xg, w_ref, part_ref):
    chunks = part_ref.shape[0]
    width = w_ref.shape[2]
    from_x = (iota((xg.shape[0], 2 * LANES), 1) & (LANES - 1)) < split
    for j in range(0, chunks, 2):
        parity = half_ref[1] if j >= chunks // 2 else 1 - half_ref[1]
        at = half_ref[0] + 2 * parity + 4 * (j % (chunks // 2))
        w = jnp.concatenate([w_ref[at], w_ref[at + 4]], axis=0)
        by_x = mm(xg[:, :width], w, ((1,), (1,)))
        by_g = mm(xg[:, width:], w, ((1,), (1,)))
        got = jnp.where(from_x, by_x, by_g).astype(bf16)
        part_ref[j] = got[:, :LANES]
        part_ref[j + 1] = got[:, LANES:]


def first_kernel(piece, split, half_ref, pack_ref, w_ref, part_ref, xg_ref):
    n_etp, rows, _ = pack_ref.shape
    slots = part_ref.shape[1]
    sel_a, sel_b = selectors(slots, rows, False)
    packed = jnp.concatenate([pack_ref[i] for i in range(n_etp)], axis=1)
    a = mm(sel_a, packed, ((1,), (0,)))
    b = mm(sel_b, packed, ((1,), (0,)))
    low = is_low(slots, 64)
    parts_x, parts_g = [], []
    for i in range(n_etp):
        at = LANES * i
        parts_x.append(a[:, at : at + piece])
        parts_g.append(a[:, at + piece : at + LANES])
        parts_g.append(jnp.where(low, b[:, at : at + 64], b[:, at + 64 : at + LANES]))
    xg = jnp.concatenate(parts_x + parts_g, axis=1).astype(bf16)
    xg_ref[...] = xg
    partials(split, half_ref, xg, w_ref, part_ref)


def second_kernel(split, half_ref, xg_ref, w_ref, part_ref):
    partials(split, half_ref, xg_ref[...], w_ref, part_ref)


def act_kernel(unit, sum_ref, head_ref, tail_ref):
    total = sum_ref[0].astype(f32)
    for j in range(1, sum_ref.shape[0]):
        total = total + sum_ref[j].astype(f32)
    keep = iota(total.shape, 1) < unit
    gate = jnp.where(keep, total, 0.0)
    up = jnp.where(keep, pltpu.roll(total, LANES - unit, 1), 0.0)
    d_hidden = jnp.where(keep, pltpu.roll(total, LANES - 2 * unit, 1), 0.0)
    sig = jax.nn.sigmoid(gate)
    hidden = gate * sig * up
    d_gate = d_hidden * up * sig * (1.0 + gate * (1.0 - sig))
    d_up = d_hidden * gate * sig
    act = d_gate + pltpu.roll(d_up, unit, 1) + pltpu.roll(hidden, 2 * unit, 1)
    act = act.astype(bf16)
    n_head = head_ref.shape[0]
    head_ref[...] = act[:n_head]
    for j in range(tail_ref.shape[0]):
        tail_ref[j] = act[n_head:]


def back_kernel(piece, split, head_ref, tail_ref, w_ref, pack_ref):
    chunks, slots = head_ref.shape[0], head_ref.shape[1] + tail_ref.shape[1]
    n_etp, rows, _ = pack_ref.shape
    width = w_ref.shape[2]
    w = w_ref[...].reshape(chunks * LANES, width)
    first = iota((1, LANES), 1) < split

    def product(keep):
        keep = jnp.where(keep, 1.0, 0.0).astype(bf16)
        act = jnp.concatenate(
            [
                jnp.concatenate([ref[j] * keep for j in range(chunks)], axis=1)
                for ref in (head_ref, tail_ref)
            ],
            axis=0,
        )
        return mm(act, w, ((1,), (0,))).astype(bf16).astype(f32)

    dx = product(first)
    y = product(jnp.logical_not(first))
    sel_a, sel_b = selectors(slots, rows, True)
    low = is_low(slots, 64)
    parts_a, parts_b = [], []
    for i in range(n_etp):
        at = piece * i
        parts_a.append(y[:, at : at + piece])
        parts_a.append(dx[:, at : at + LANES - piece])
        tail = dx[:, at + LANES - piece : at + piece]
        parts_b.append(jnp.where(low, tail, 0.0))
        parts_b.append(jnp.where(low, 0.0, tail))
    a = jnp.concatenate(parts_a, axis=1).astype(bf16)
    b = jnp.concatenate(parts_b, axis=1).astype(bf16)
    packed = (mm(sel_a, a, ((1,), (0,))) + mm(sel_b, b, ((1,), (0,)))).astype(bf16)
    for i in range(n_etp):
        pack_ref[i] = packed[:, LANES * i : LANES * (i + 1)]


def combine_kernel(
    piece, weight_ref, place_ref, place_b_ref, place_c_ref, back_ref, out_ref, grad_ref
):
    back = back_ref[...]
    rest = weight_ref[...]
    total = None
    for _ in range(3):
        high = rest.astype(bf16)
        rest = rest - high.astype(f32)
        term = mm(high, back, ((0,), (0,)))
        total = term if total is None else total + term
    out_ref[...] = total[:, :piece].astype(bf16)
    a = mm(place_ref[...], back, ((0,), (0,)))
    b = mm(place_b_ref[...], back, ((0,), (0,)))
    c = mm(place_c_ref[...], back, ((0,), (0,)))
    grad_ref[...] = jnp.concatenate(
        [a[:, piece:LANES], b[:, :64] + c[:, 64:]], axis=1
    ).astype(bf16)


def local(tokens, routes, combine_weights, gate_weight, up_weight, down_weight, out_cotangent):
    block_len, top_count = routes.shape
    n_exp = lax.axis_size("expert")
    n_etp = lax.axis_size("etp")
    n_dp = lax.axis_size("dp")
    n_y = n_dp // 2
    width = tokens.shape[1]
    piece = width // n_etp
    hid = gate_weight.shape[2]
    unit = hid // n_dp
    slots = n_exp * CAP
    rows = n_exp * PACK
    same_parity = [[4 * k + i for k in range(n_y // 2)] for i in range(4)]
    other_core = [(i, i ^ 1) for i in range(n_dp)]
    core = lax.bitwise_and(lax.axis_index("dp"), 1)
    parity = lax.bitwise_and(lax.shift_right_logical(lax.axis_index("dp"), 1), 1)
    mine, theirs = jnp.stack([core, parity]), jnp.stack([1 - core, parity])
    col = lax.axis_index("etp") * piece

    send, place, place_b, place_c, weight = call(
        functools.partial(dispatch_kernel, piece),
        [
            ((rows, LANES), bf16),
            ((rows, block_len), bf16),
            ((rows, block_len), bf16),
            ((rows, block_len), bf16),
            ((rows, block_len), f32),
        ],
        60_000_000,
        1,
        col[None],
        tokens,
        out_cotangent,
        routes.T,
        combine_weights.T,
        far=True,
        room=60,
        scratch=[
            pltpu.VMEM(tokens.shape, bf16),
            pltpu.VMEM(out_cotangent.shape, bf16),
            pltpu.VMEM((top_count, block_len), jnp.int32),
            pltpu.VMEM((top_count, block_len), f32),
            pltpu.SemaphoreType.DMA((4,)),
        ],
    )
    send, gate_weight, up_weight, down_weight = lax.optimization_barrier(
        (send, gate_weight, up_weight, down_weight)
    )
    w_gate = gate_weight[0].T.reshape(n_dp, unit, width)
    w_up = up_weight[0].T.reshape(n_dp, unit, width)
    w_down = down_weight[0].reshape(n_dp, unit, width)
    spare = LANES - 3 * unit

    w_front = jnp.concatenate(
        [w_gate, w_up, w_down, jnp.zeros((n_dp, spare, width), bf16)], axis=1
    )

    got = swap(send.reshape(n_exp, PACK, LANES), "expert").reshape(1, rows, LANES)
    got, w_front = lax.optimization_barrier((got, w_front))
    packs = swap(jnp.broadcast_to(got, (n_etp, rows, LANES)), "etp")

    half_flops = 2 * slots * 2 * width * n_y * LANES
    part_shape = ((n_y, slots, LANES), bf16)
    part_theirs, xg = call(
        functools.partial(first_kernel, piece, 2 * unit),
        [part_shape, ((slots, 2 * width), bf16)],
        2 * half_flops,
        1,
        theirs,
        packs,
        w_front,
    )
    arrived = lax.ppermute(part_theirs, "dp", other_core)
    (part_mine,) = call(
        functools.partial(second_kernel, 2 * unit), [part_shape], half_flops, 1, mine, xg, w_front)
    cut = n_y // 2
    away = (part_mine[:cut].astype(f32) + arrived[:cut].astype(f32)).astype(bf16)
    away = lax.ppermute(away, "dp", [(i, i ^ 2) for i in range(n_dp)])
    kept = part_mine[cut:].astype(f32) + arrived[cut:].astype(f32)
    kept = (kept + away.astype(f32)).astype(bf16)
    head, tail = call(
        functools.partial(act_kernel, unit),
        [((HEAD, LANES), bf16), ((n_dp, slots - HEAD, LANES), bf16)],
        10_000_000,
        0,
        swap(kept, "dp", same_parity),
    )
    tail = swap(tail, "dp")
    head = lax.all_gather(head, "dp", axis=0)
    (out,) = call(
        functools.partial(back_kernel, piece, 2 * unit),
        [((n_etp, rows, LANES), bf16)],
        4 * half_flops,
        0,
        head,
        tail,
        w_front,
    )
    out = jnp.sum(swap(out, "etp").astype(f32), axis=0).astype(bf16)
    back = swap(out.reshape(n_exp, PACK, LANES), "expert").reshape(rows, LANES)

    full = jnp.concatenate([head, tail], axis=1)
    grads = mm(full, xg, ((1,), (0,))).astype(bf16)

    def take(start, at):
        return grads[:, start : start + unit, at : at + width].reshape(hid, width)

    gate_grad = take(0, 0).T
    up_grad = take(unit, 0).T
    down_grad = take(2 * unit, width)
    layer_output, tokens_grad = call(
        functools.partial(combine_kernel, piece),
        [((block_len, piece), bf16), ((block_len, piece), bf16)],
        50_000_000,
        0,
        weight,
        place,
        place_b,
        place_c,
        back,
    )
    return layer_output, tokens_grad, gate_grad[None], up_grad[None], down_grad[None]


def solution(mesh):
    placed = (
        P("expert", "dp"),
        P("expert", None),
        P("expert", None),
        P("expert", "dp", "etp"),
        P("expert", "dp", "etp"),
        P("expert", "etp", "dp"),
        P("expert", "dp"),
    )
    return jax.shard_map(
        local,
        mesh=mesh,
        in_specs=placed,
        out_specs=(
            P("expert", ("dp", "etp")),
            P("expert", ("dp", "etp")),
            P("expert", "dp", "etp"),
            P("expert", "dp", "etp"),
            P("expert", "etp", "dp"),
        ),
        check_vma=False,
    )
```

```python
import functools

import jax
import jax.numpy as jnp
from jax import lax
from jax.experimental import pallas as pl
from jax.experimental.pallas import tpu as pltpu
from jax.sharding import PartitionSpec as P

LANES = 128
f32 = jnp.float32
bf16 = jnp.bfloat16


def mm(left, right, dims):
    return lax.dot_general(left, right, (dims, ((), ())), preferred_element_type=f32)


def swap(x, axis, groups=None):
    return lax.all_to_all(
        x, axis, split_axis=0, concat_axis=0, tiled=True, axis_index_groups=groups
    )


def far_order(count):
    return [(k >> 1) + (count // 2) * (k & 1) for k in range(count)]


def iota(shape, axis):
    return lax.broadcasted_iota(jnp.int32, shape, axis)


def call(kernel, outs, flops, n_scalar, *args, far=False, scratch=(), room=16):
    smem = pl.BlockSpec(memory_space=pltpu.SMEM)
    vmem = pl.BlockSpec(memory_space=pltpu.VMEM)
    held = pl.BlockSpec(memory_space=pltpu.HBM) if far else vmem
    outs = [jax.ShapeDtypeStruct(*o) for o in outs]
    moved = sum(a.size * a.dtype.itemsize for a in (*args, *outs))
    return pl.pallas_call(
        kernel,
        out_shape=outs,
        in_specs=[smem] * n_scalar + [held] * (len(args) - n_scalar),
        out_specs=[vmem] * len(outs),
        scratch_shapes=list(scratch),
        compiler_params=pltpu.CompilerParams(vmem_limit_bytes=room * 1024 * 1024),
        cost_estimate=pl.CostEstimate(flops=flops, bytes_accessed=moved, transcendentals=0),
    )(*args)


CAP = 21
PACK = 32
FOLD = PACK - CAP
HEAD = 240


def dispatch_kernel(
    piece,
    col_ref,
    tok_hbm,
    cot_hbm,
    route_hbm,
    cw_hbm,
    send_ref,
    place_ref,
    place_b_ref,
    place_c_ref,
    weight_ref,
    tok_ref,
    cot_ref,
    route_ref,
    cw_ref,
    sems,
):
    pairs = ((route_hbm, route_ref), (cw_hbm, cw_ref), (tok_hbm, tok_ref), (cot_hbm, cot_ref))
    copies = [pltpu.make_async_copy(a, b, sems.at[i]) for i, (a, b) in enumerate(pairs)]
    for copy in copies:
        copy.start()
    copies[0].wait()
    copies[1].wait()
    width = tok_ref.shape[1]
    top_count, block_len = route_ref.shape
    rows = send_ref.shape[0]
    row = iota((rows, block_len), 0)
    place_in_ring = lax.shift_right_logical(row, 5)
    owner = lax.shift_right_logical(place_in_ring, 1) + (place_in_ring & 1) * (rows // PACK // 2)
    inner = row & (PACK - 1)
    hit = jnp.zeros((rows, block_len), f32)
    weight = jnp.zeros((rows, block_len), f32)
    for k in range(top_count):
        hit_k = owner == route_ref[k : k + 1, :]
        hit = jnp.where(hit_k, 1.0, hit)
        weight = jnp.where(hit_k, cw_ref[k : k + 1, :], weight)
    square = (block_len, block_len)
    earlier = jnp.where(iota(square, 0) < iota(square, 1), 1.0, 0.0).astype(bf16)
    before = mm(hit.astype(bf16), earlier, ((1,), (0,)))
    inner_f = inner.astype(f32)
    folded = jnp.where(inner >= CAP, hit, 0.0)
    place = jnp.where((before == inner_f) & (inner < CAP), hit, 0.0)
    place_b = jnp.where(before == inner_f - CAP, folded, 0.0)
    place_c = jnp.where(before == inner_f - (CAP - FOLD), folded, 0.0)
    place_ref[...] = place.astype(bf16)
    place_b_ref[...] = place_b.astype(bf16)
    place_c_ref[...] = place_c.astype(bf16)
    weight_ref[...] = weight * place
    pick_row = iota((width, LANES), 0) - col_ref[0]
    lane = iota((width, LANES), 1)
    pick_x = jnp.where((pick_row == lane) & (lane < piece), 1.0, 0.0).astype(bf16)
    pick_g = jnp.where((pick_row == lane - piece) & (lane >= piece), 1.0, 0.0).astype(bf16)
    rest = (lane & 63) + (LANES - piece)
    pick_r = jnp.where(pick_row == rest, 1.0, 0.0).astype(bf16)
    copies[2].wait()
    copies[3].wait()
    cot = cot_ref[...]
    first = mm(tok_ref[...], pick_x, ((1,), (0,))) + mm(cot, pick_g, ((1,), (0,)))
    last = mm(cot, pick_r, ((1,), (0,))).astype(bf16)
    lanes = iota((rows, LANES), 1)
    scale = jnp.sum(weight * place, axis=1, keepdims=True)
    scale_b = jnp.sum(weight * place_b, axis=1, keepdims=True)
    scale_c = jnp.sum(weight * place_c, axis=1, keepdims=True)
    a = mm(place.astype(bf16), first.astype(bf16), ((1,), (0,)))
    b = mm(place_b.astype(bf16), last, ((1,), (0,)))
    c = mm(place_c.astype(bf16), last, ((1,), (0,)))
    a = jnp.where(lanes < piece, a, a * scale)
    send_ref[...] = (a + jnp.where(lanes < 64, b * scale_b, c * scale_c)).astype(bf16)


def selectors(slots, rows, flip):
    shape, slot_axis = ((rows, slots), 1) if flip else ((slots, rows), 0)
    slot = iota(shape, slot_axis)
    row = iota(shape, 1 - slot_axis)
    base = lax.shift_right_logical(row, 5) * CAP
    inner = row & (PACK - 1)
    at = slot - base
    sel_a = jnp.where((at == inner) & (inner < CAP), 1.0, 0.0).astype(bf16)
    low = at == inner - CAP
    high = (at == inner - (CAP - FOLD)) & (inner < PACK - 1)
    sel_b = jnp.where((low | high) & (inner >= CAP), 1.0, 0.0).astype(bf16)
    return sel_a, sel_b


def is_low(slots, lanes):
    slot = iota((slots, lanes), 0)
    rank = slot - lax.shift_right_logical(slot * 3121, 16) * CAP
    return rank < FOLD


def partials(split, half_ref, xg, w_ref, part_ref):
    chunks = part_ref.shape[0]
    width = w_ref.shape[2]
    from_x = (iota((xg.shape[0], 2 * LANES), 1) & (LANES - 1)) < split
    for j in range(0, chunks, 2):
        order = far_order(chunks)
        at, after = half_ref[0] + 2 * order[j], half_ref[0] + 2 * order[j + 1]
        w = jnp.concatenate([w_ref[at], w_ref[after]], axis=0)
        by_x = mm(xg[:, :width], w, ((1,), (1,)))
        by_g = mm(xg[:, width:], w, ((1,), (1,)))
        got = jnp.where(from_x, by_x, by_g).astype(bf16)
        part_ref[j] = got[:, :LANES]
        part_ref[j + 1] = got[:, LANES:]


def first_kernel(piece, split, half_ref, pack_ref, w_ref, part_ref, xg_ref):
    n_etp, rows, _ = pack_ref.shape
    slots = part_ref.shape[1]
    sel_a, sel_b = selectors(slots, rows, False)
    packed = jnp.concatenate([pack_ref[i] for i in range(n_etp)], axis=1)
    a = mm(sel_a, packed, ((1,), (0,)))
    b = mm(sel_b, packed, ((1,), (0,)))
    low = is_low(slots, 64)
    parts_x, parts_g = [], []
    for i in range(n_etp):
        at = LANES * i
        parts_x.append(a[:, at : at + piece])
        parts_g.append(a[:, at + piece : at + LANES])
        parts_g.append(jnp.where(low, b[:, at : at + 64], b[:, at + 64 : at + LANES]))
    xg = jnp.concatenate(parts_x + parts_g, axis=1).astype(bf16)
    xg_ref[...] = xg
    partials(split, half_ref, xg, w_ref, part_ref)


def second_kernel(split, half_ref, xg_ref, w_ref, part_ref):
    partials(split, half_ref, xg_ref[...], w_ref, part_ref)


def act_kernel(unit, sum_ref, head_ref, tail_ref):
    total = sum_ref[0].astype(f32)
    for j in range(1, sum_ref.shape[0]):
        total = total + sum_ref[j].astype(f32)
    keep = iota(total.shape, 1) < unit
    gate = jnp.where(keep, total, 0.0)
    up = jnp.where(keep, pltpu.roll(total, LANES - unit, 1), 0.0)
    d_hidden = jnp.where(keep, pltpu.roll(total, LANES - 2 * unit, 1), 0.0)
    sig = jax.nn.sigmoid(gate)
    hidden = gate * sig * up
    d_gate = d_hidden * up * sig * (1.0 + gate * (1.0 - sig))
    d_up = d_hidden * gate * sig
    act = d_gate + pltpu.roll(d_up, unit, 1) + pltpu.roll(hidden, 2 * unit, 1)
    act = act.astype(bf16)
    n_head = head_ref.shape[0]
    head_ref[...] = act[:n_head]
    for j in range(tail_ref.shape[0]):
        tail_ref[j] = act[n_head:]


def back_kernel(piece, split, head_ref, tail_ref, w_ref, pack_ref):
    chunks, slots = head_ref.shape[0], head_ref.shape[1] + tail_ref.shape[1]
    n_etp, rows, _ = pack_ref.shape
    width = w_ref.shape[2]
    w = w_ref[...].reshape(chunks * LANES, width)
    first = iota((1, LANES), 1) < split

    def product(keep):
        keep = jnp.where(keep, 1.0, 0.0).astype(bf16)
        act = jnp.concatenate(
            [
                jnp.concatenate([ref[j] * keep for j in range(chunks)], axis=1)
                for ref in (head_ref, tail_ref)
            ],
            axis=0,
        )
        return mm(act, w, ((1,), (0,))).astype(bf16).astype(f32)

    dx = product(first)
    y = product(jnp.logical_not(first))
    sel_a, sel_b = selectors(slots, rows, True)
    low = is_low(slots, 64)
    parts_a, parts_b = [], []
    for i in range(n_etp):
        at = piece * i
        parts_a.append(y[:, at : at + piece])
        parts_a.append(dx[:, at : at + LANES - piece])
        tail = dx[:, at + LANES - piece : at + piece]
        parts_b.append(jnp.where(low, tail, 0.0))
        parts_b.append(jnp.where(low, 0.0, tail))
    a = jnp.concatenate(parts_a, axis=1).astype(bf16)
    b = jnp.concatenate(parts_b, axis=1).astype(bf16)
    packed = (mm(sel_a, a, ((1,), (0,))) + mm(sel_b, b, ((1,), (0,)))).astype(bf16)
    for i in range(n_etp):
        pack_ref[i] = packed[:, LANES * i : LANES * (i + 1)]


def combine_kernel(
    piece, weight_ref, place_ref, place_b_ref, place_c_ref, back_ref, out_ref, grad_ref
):
    back = back_ref[...]
    rest = weight_ref[...]
    total = None
    for _ in range(3):
        high = rest.astype(bf16)
        rest = rest - high.astype(f32)
        term = mm(high, back, ((0,), (0,)))
        total = term if total is None else total + term
    out_ref[...] = total[:, :piece].astype(bf16)
    a = mm(place_ref[...], back, ((0,), (0,)))
    b = mm(place_b_ref[...], back, ((0,), (0,)))
    c = mm(place_c_ref[...], back, ((0,), (0,)))
    grad_ref[...] = jnp.concatenate(
        [a[:, piece:LANES], b[:, :64] + c[:, 64:]], axis=1
    ).astype(bf16)


def local(tokens, routes, combine_weights, gate_weight, up_weight, down_weight, out_cotangent):
    block_len, top_count = routes.shape
    n_exp = lax.axis_size("expert")
    n_etp = lax.axis_size("etp")
    n_dp = lax.axis_size("dp")
    n_y = n_dp // 2
    width = tokens.shape[1]
    piece = width // n_etp
    hid = gate_weight.shape[2]
    unit = hid // n_dp
    slots = n_exp * CAP
    rows = n_exp * PACK
    same_core = [[2 * y + c for y in far_order(n_y)] for c in range(2)]
    other_core = [(i, i ^ 1) for i in range(n_dp)]
    experts = [far_order(n_exp)]
    core = lax.bitwise_and(lax.axis_index("dp"), 1)
    mine, theirs = core[None], (1 - core)[None]
    col = lax.axis_index("etp") * piece

    send, place, place_b, place_c, weight = call(
        functools.partial(dispatch_kernel, piece),
        [
            ((rows, LANES), bf16),
            ((rows, block_len), bf16),
            ((rows, block_len), bf16),
            ((rows, block_len), bf16),
            ((rows, block_len), f32),
        ],
        60_000_000,
        1,
        col[None],
        tokens,
        out_cotangent,
        routes.T,
        combine_weights.T,
        far=True,
        room=60,
        scratch=[
            pltpu.VMEM(tokens.shape, bf16),
            pltpu.VMEM(out_cotangent.shape, bf16),
            pltpu.VMEM((top_count, block_len), jnp.int32),
            pltpu.VMEM((top_count, block_len), f32),
            pltpu.SemaphoreType.DMA((4,)),
        ],
    )
    send, gate_weight, up_weight, down_weight = lax.optimization_barrier(
        (send, gate_weight, up_weight, down_weight)
    )
    w_gate = gate_weight[0].T.reshape(n_dp, unit, width)
    w_up = up_weight[0].T.reshape(n_dp, unit, width)
    w_down = down_weight[0].reshape(n_dp, unit, width)
    spare = LANES - 3 * unit

    w_front = jnp.concatenate(
        [w_gate, w_up, w_down, jnp.zeros((n_dp, spare, width), bf16)], axis=1
    )

    got = swap(send.reshape(n_exp, PACK, LANES), "expert", experts).reshape(1, rows, LANES)
    got, w_front = lax.optimization_barrier((got, w_front))
    packs = swap(jnp.broadcast_to(got, (n_etp, rows, LANES)), "etp")

    half_flops = 2 * slots * 2 * width * n_y * LANES
    part_shape = ((n_y, slots, LANES), bf16)
    part_theirs, xg = call(
        functools.partial(first_kernel, piece, 2 * unit),
        [part_shape, ((slots, 2 * width), bf16)],
        2 * half_flops,
        1,
        theirs,
        packs,
        w_front,
    )
    arrived = lax.ppermute(part_theirs, "dp", other_core)
    (part_mine,) = call(
        functools.partial(second_kernel, 2 * unit), [part_shape], half_flops, 1, mine, xg, w_front)
    chip = (part_mine.astype(f32) + arrived.astype(f32)).astype(bf16)
    head, tail = call(
        functools.partial(act_kernel, unit),
        [((HEAD, LANES), bf16), ((n_dp, slots - HEAD, LANES), bf16)],
        10_000_000,
        0,
        swap(chip, "dp", same_core),
    )
    tail = swap(tail, "dp")
    head = lax.all_gather(head, "dp", axis=0)
    (out,) = call(
        functools.partial(back_kernel, piece, 2 * unit),
        [((n_etp, rows, LANES), bf16)],
        4 * half_flops,
        0,
        head,
        tail,
        w_front,
    )
    out = jnp.sum(swap(out, "etp").astype(f32), axis=0).astype(bf16)
    back = swap(out.reshape(n_exp, PACK, LANES), "expert", experts).reshape(rows, LANES)

    full = jnp.concatenate([head, tail], axis=1)
    grads = mm(full, xg, ((1,), (0,))).astype(bf16)

    def take(start, at):
        return grads[:, start : start + unit, at : at + width].reshape(hid, width)

    gate_grad = take(0, 0).T
    up_grad = take(unit, 0).T
    down_grad = take(2 * unit, width)
    layer_output, tokens_grad = call(
        functools.partial(combine_kernel, piece),
        [((block_len, piece), bf16), ((block_len, piece), bf16)],
        50_000_000,
        0,
        weight,
        place,
        place_b,
        place_c,
        back,
    )
    return layer_output, tokens_grad, gate_grad[None], up_grad[None], down_grad[None]


def solution(mesh):
    placed = (
        P("expert", "dp"),
        P("expert", None),
        P("expert", None),
        P("expert", "dp", "etp"),
        P("expert", "dp", "etp"),
        P("expert", "etp", "dp"),
        P("expert", "dp"),
    )
    return jax.shard_map(
        local,
        mesh=mesh,
        in_specs=placed,
        out_specs=(
            P("expert", ("dp", "etp")),
            P("expert", ("dp", "etp")),
            P("expert", "dp", "etp"),
            P("expert", "dp", "etp"),
            P("expert", "etp", "dp"),
        ),
        check_vma=False,
    )
```

```python
import functools

import jax
import jax.numpy as jnp
from jax import lax
from jax.experimental import pallas as pl
from jax.experimental.pallas import tpu as pltpu
from jax.sharding import PartitionSpec as P

LANES = 128
f32 = jnp.float32
bf16 = jnp.bfloat16


def mm(left, right, dims):
    return lax.dot_general(left, right, (dims, ((), ())), preferred_element_type=f32)


def swap(x, axis, groups=None):
    return lax.all_to_all(
        x, axis, split_axis=0, concat_axis=0, tiled=True, axis_index_groups=groups
    )


def far_order(count):
    return [(k >> 1) + (count // 2) * (k & 1) for k in range(count)]


def iota(shape, axis):
    return lax.broadcasted_iota(jnp.int32, shape, axis)


def call(kernel, outs, flops, n_scalar, *args, far=False, scratch=(), room=16):
    smem = pl.BlockSpec(memory_space=pltpu.SMEM)
    vmem = pl.BlockSpec(memory_space=pltpu.VMEM)
    held = pl.BlockSpec(memory_space=pltpu.HBM) if far else vmem
    outs = [jax.ShapeDtypeStruct(*o) for o in outs]
    moved = sum(a.size * a.dtype.itemsize for a in (*args, *outs))
    return pl.pallas_call(
        kernel,
        out_shape=outs,
        in_specs=[smem] * n_scalar + [held] * (len(args) - n_scalar),
        out_specs=[vmem] * len(outs),
        scratch_shapes=list(scratch),
        compiler_params=pltpu.CompilerParams(vmem_limit_bytes=room * 1024 * 1024),
        cost_estimate=pl.CostEstimate(flops=flops, bytes_accessed=moved, transcendentals=0),
    )(*args)


CAP = 21
PACK = 32
FOLD = PACK - CAP
HEAD = 240


def dispatch_kernel(
    piece,
    col_ref,
    tok_hbm,
    cot_hbm,
    route_hbm,
    cw_hbm,
    send_ref,
    place_ref,
    place_b_ref,
    place_c_ref,
    weight_ref,
    tok_ref,
    cot_ref,
    route_ref,
    cw_ref,
    sems,
):
    pairs = ((route_hbm, route_ref), (cw_hbm, cw_ref), (tok_hbm, tok_ref), (cot_hbm, cot_ref))
    copies = [pltpu.make_async_copy(a, b, sems.at[i]) for i, (a, b) in enumerate(pairs)]
    for copy in copies:
        copy.start()
    copies[0].wait()
    copies[1].wait()
    width = tok_ref.shape[1]
    top_count, block_len = route_ref.shape
    rows = send_ref.shape[0]
    row = iota((rows, block_len), 0)
    place_in_ring = lax.shift_right_logical(row, 5)
    owner = lax.shift_right_logical(place_in_ring, 1) + (place_in_ring & 1) * (rows // PACK // 2)
    inner = row & (PACK - 1)
    hit = jnp.zeros((rows, block_len), f32)
    weight = jnp.zeros((rows, block_len), f32)
    for k in range(top_count):
        hit_k = owner == route_ref[k : k + 1, :]
        hit = jnp.where(hit_k, 1.0, hit)
        weight = jnp.where(hit_k, cw_ref[k : k + 1, :], weight)
    square = (block_len, block_len)
    earlier = jnp.where(iota(square, 0) < iota(square, 1), 1.0, 0.0).astype(bf16)
    before = mm(hit.astype(bf16), earlier, ((1,), (0,)))
    inner_f = inner.astype(f32)
    folded = jnp.where(inner >= CAP, hit, 0.0)
    place = jnp.where((before == inner_f) & (inner < CAP), hit, 0.0)
    place_b = jnp.where(before == inner_f - CAP, folded, 0.0)
    place_c = jnp.where(before == inner_f - (CAP - FOLD), folded, 0.0)
    place_ref[...] = place.astype(bf16)
    place_b_ref[...] = place_b.astype(bf16)
    place_c_ref[...] = place_c.astype(bf16)
    weight_ref[...] = weight * place
    pick_row = iota((width, LANES), 0) - col_ref[0]
    lane = iota((width, LANES), 1)
    pick_x = jnp.where((pick_row == lane) & (lane < piece), 1.0, 0.0).astype(bf16)
    pick_g = jnp.where((pick_row == lane - piece) & (lane >= piece), 1.0, 0.0).astype(bf16)
    rest = (lane & 63) + (LANES - piece)
    pick_r = jnp.where(pick_row == rest, 1.0, 0.0).astype(bf16)
    copies[2].wait()
    copies[3].wait()
    cot = cot_ref[...]
    first = mm(tok_ref[...], pick_x, ((1,), (0,))) + mm(cot, pick_g, ((1,), (0,)))
    last = mm(cot, pick_r, ((1,), (0,))).astype(bf16)
    lanes = iota((rows, LANES), 1)
    scale = jnp.sum(weight * place, axis=1, keepdims=True)
    scale_b = jnp.sum(weight * place_b, axis=1, keepdims=True)
    scale_c = jnp.sum(weight * place_c, axis=1, keepdims=True)
    a = mm(place.astype(bf16), first.astype(bf16), ((1,), (0,)))
    b = mm(place_b.astype(bf16), last, ((1,), (0,)))
    c = mm(place_c.astype(bf16), last, ((1,), (0,)))
    a = jnp.where(lanes < piece, a, a * scale)
    send_ref[...] = (a + jnp.where(lanes < 64, b * scale_b, c * scale_c)).astype(bf16)


def selectors(slots, rows, flip):
    shape, slot_axis = ((rows, slots), 1) if flip else ((slots, rows), 0)
    slot = iota(shape, slot_axis)
    row = iota(shape, 1 - slot_axis)
    base = lax.shift_right_logical(row, 5) * CAP
    inner = row & (PACK - 1)
    at = slot - base
    sel_a = jnp.where((at == inner) & (inner < CAP), 1.0, 0.0).astype(bf16)
    low = at == inner - CAP
    high = (at == inner - (CAP - FOLD)) & (inner < PACK - 1)
    sel_b = jnp.where((low | high) & (inner >= CAP), 1.0, 0.0).astype(bf16)
    return sel_a, sel_b


def is_low(slots, lanes):
    slot = iota((slots, lanes), 0)
    rank = slot - lax.shift_right_logical(slot * 3121, 16) * CAP
    return rank < FOLD


def partials(split, half_ref, xg, w_ref, part_ref):
    chunks = part_ref.shape[0]
    width = w_ref.shape[2]
    from_x = (iota((xg.shape[0], 2 * LANES), 1) & (LANES - 1)) < split
    for j in range(0, chunks, 2):
        order = far_order(chunks)
        at, after = half_ref[0] + 2 * order[j], half_ref[0] + 2 * order[j + 1]
        w = jnp.concatenate([w_ref[at], w_ref[after]], axis=0)
        by_x = mm(xg[:, :width], w, ((1,), (1,)))
        by_g = mm(xg[:, width:], w, ((1,), (1,)))
        got = jnp.where(from_x, by_x, by_g).astype(bf16)
        part_ref[j] = got[:, :LANES]
        part_ref[j + 1] = got[:, LANES:]


def first_kernel(piece, split, half_ref, pack_ref, w_ref, part_ref, xg_ref):
    n_etp, rows, _ = pack_ref.shape
    slots = part_ref.shape[1]
    sel_a, sel_b = selectors(slots, rows, False)
    packed = jnp.concatenate([pack_ref[i] for i in range(n_etp)], axis=1)
    a = mm(sel_a, packed, ((1,), (0,)))
    b = mm(sel_b, packed, ((1,), (0,)))
    low = is_low(slots, 64)
    parts_x, parts_g = [], []
    for i in range(n_etp):
        at = LANES * i
        parts_x.append(a[:, at : at + piece])
        parts_g.append(a[:, at + piece : at + LANES])
        parts_g.append(jnp.where(low, b[:, at : at + 64], b[:, at + 64 : at + LANES]))
    xg = jnp.concatenate(parts_x + parts_g, axis=1).astype(bf16)
    xg_ref[...] = xg
    partials(split, half_ref, xg, w_ref, part_ref)


def second_kernel(split, half_ref, xg_ref, w_ref, part_ref):
    partials(split, half_ref, xg_ref[...], w_ref, part_ref)


def act_kernel(unit, sum_ref, head_ref, tail_ref):
    total = sum_ref[0].astype(f32)
    for j in range(1, sum_ref.shape[0]):
        total = total + sum_ref[j].astype(f32)
    keep = iota(total.shape, 1) < unit
    gate = jnp.where(keep, total, 0.0)
    up = jnp.where(keep, pltpu.roll(total, LANES - unit, 1), 0.0)
    d_hidden = jnp.where(keep, pltpu.roll(total, LANES - 2 * unit, 1), 0.0)
    sig = jax.nn.sigmoid(gate)
    hidden = gate * sig * up
    d_gate = d_hidden * up * sig * (1.0 + gate * (1.0 - sig))
    d_up = d_hidden * gate * sig
    act = d_gate + pltpu.roll(d_up, unit, 1) + pltpu.roll(hidden, 2 * unit, 1)
    act = act.astype(bf16)
    n_head = head_ref.shape[0]
    head_ref[...] = act[:n_head]
    for j in range(tail_ref.shape[0]):
        tail_ref[j] = act[n_head:]


def back_kernel(piece, split, head_ref, tail_ref, w_ref, pack_ref):
    chunks, slots = head_ref.shape[0], head_ref.shape[1] + tail_ref.shape[1]
    n_etp, rows, _ = pack_ref.shape
    width = w_ref.shape[2]
    w = w_ref[...].reshape(chunks * LANES, width)
    first = iota((1, LANES), 1) < split
    arrival = far_order(chunks)

    def product(keep):
        keep = jnp.where(keep, 1.0, 0.0).astype(bf16)
        act = jnp.concatenate(
            [
                jnp.concatenate([ref[at(j)] * keep for j in range(chunks)], axis=1)
                for ref, at in ((head_ref, int), (tail_ref, arrival.index))
            ],
            axis=0,
        )
        return mm(act, w, ((1,), (0,))).astype(bf16).astype(f32)

    dx = product(first)
    y = product(jnp.logical_not(first))
    sel_a, sel_b = selectors(slots, rows, True)
    low = is_low(slots, 64)
    parts_a, parts_b = [], []
    for i in range(n_etp):
        at = piece * i
        parts_a.append(y[:, at : at + piece])
        parts_a.append(dx[:, at : at + LANES - piece])
        tail = dx[:, at + LANES - piece : at + piece]
        parts_b.append(jnp.where(low, tail, 0.0))
        parts_b.append(jnp.where(low, 0.0, tail))
    a = jnp.concatenate(parts_a, axis=1).astype(bf16)
    b = jnp.concatenate(parts_b, axis=1).astype(bf16)
    packed = (mm(sel_a, a, ((1,), (0,))) + mm(sel_b, b, ((1,), (0,)))).astype(bf16)
    for i in range(n_etp):
        pack_ref[i] = packed[:, LANES * i : LANES * (i + 1)]


def combine_kernel(
    piece, weight_ref, place_ref, place_b_ref, place_c_ref, back_ref, out_ref, grad_ref
):
    back = back_ref[...]
    rest = weight_ref[...]
    total = None
    for _ in range(3):
        high = rest.astype(bf16)
        rest = rest - high.astype(f32)
        term = mm(high, back, ((0,), (0,)))
        total = term if total is None else total + term
    out_ref[...] = total[:, :piece].astype(bf16)
    a = mm(place_ref[...], back, ((0,), (0,)))
    b = mm(place_b_ref[...], back, ((0,), (0,)))
    c = mm(place_c_ref[...], back, ((0,), (0,)))
    grad_ref[...] = jnp.concatenate(
        [a[:, piece:LANES], b[:, :64] + c[:, 64:]], axis=1
    ).astype(bf16)


def local(tokens, routes, combine_weights, gate_weight, up_weight, down_weight, out_cotangent):
    block_len, top_count = routes.shape
    n_exp = lax.axis_size("expert")
    n_etp = lax.axis_size("etp")
    n_dp = lax.axis_size("dp")
    n_y = n_dp // 2
    width = tokens.shape[1]
    piece = width // n_etp
    hid = gate_weight.shape[2]
    unit = hid // n_dp
    slots = n_exp * CAP
    rows = n_exp * PACK
    same_core = [[2 * y + c for y in far_order(n_y)] for c in range(2)]
    other_core = [(i, i ^ 1) for i in range(n_dp)]
    experts = [far_order(n_exp)]
    core = lax.bitwise_and(lax.axis_index("dp"), 1)
    mine, theirs = core[None], (1 - core)[None]
    col = lax.axis_index("etp") * piece

    send, place, place_b, place_c, weight = call(
        functools.partial(dispatch_kernel, piece),
        [
            ((rows, LANES), bf16),
            ((rows, block_len), bf16),
            ((rows, block_len), bf16),
            ((rows, block_len), bf16),
            ((rows, block_len), f32),
        ],
        60_000_000,
        1,
        col[None],
        tokens,
        out_cotangent,
        routes.T,
        combine_weights.T,
        far=True,
        room=60,
        scratch=[
            pltpu.VMEM(tokens.shape, bf16),
            pltpu.VMEM(out_cotangent.shape, bf16),
            pltpu.VMEM((top_count, block_len), jnp.int32),
            pltpu.VMEM((top_count, block_len), f32),
            pltpu.SemaphoreType.DMA((4,)),
        ],
    )
    send, gate_weight, up_weight, down_weight = lax.optimization_barrier(
        (send, gate_weight, up_weight, down_weight)
    )
    w_gate = gate_weight[0].T.reshape(n_dp, unit, width)
    w_up = up_weight[0].T.reshape(n_dp, unit, width)
    w_down = down_weight[0].reshape(n_dp, unit, width)
    spare = LANES - 3 * unit

    w_front = jnp.concatenate(
        [w_gate, w_up, w_down, jnp.zeros((n_dp, spare, width), bf16)], axis=1
    )

    got = swap(send.reshape(n_exp, PACK, LANES), "expert", experts).reshape(1, rows, LANES)
    got, w_front = lax.optimization_barrier((got, w_front))
    packs = swap(jnp.broadcast_to(got, (n_etp, rows, LANES)), "etp")

    half_flops = 2 * slots * 2 * width * n_y * LANES
    part_shape = ((n_y, slots, LANES), bf16)
    part_theirs, xg = call(
        functools.partial(first_kernel, piece, 2 * unit),
        [part_shape, ((slots, 2 * width), bf16)],
        2 * half_flops,
        1,
        theirs,
        packs,
        w_front,
    )
    arrived = lax.ppermute(part_theirs, "dp", other_core)
    (part_mine,) = call(
        functools.partial(second_kernel, 2 * unit), [part_shape], half_flops, 1, mine, xg, w_front)
    chip = (part_mine.astype(f32) + arrived.astype(f32)).astype(bf16)
    head, tail = call(
        functools.partial(act_kernel, unit),
        [((HEAD, LANES), bf16), ((n_dp, slots - HEAD, LANES), bf16)],
        10_000_000,
        0,
        swap(chip, "dp", same_core),
    )
    tail = swap(tail, "dp", [far_order(n_dp)])
    head = lax.all_gather(head, "dp", axis=0)
    (out,) = call(
        functools.partial(back_kernel, piece, 2 * unit),
        [((n_etp, rows, LANES), bf16)],
        4 * half_flops,
        0,
        head,
        tail,
        w_front,
    )
    out = jnp.sum(swap(out, "etp").astype(f32), axis=0).astype(bf16)
    back = swap(out.reshape(n_exp, PACK, LANES), "expert", experts).reshape(rows, LANES)

    in_place = jnp.stack([tail[far_order(n_dp).index(j)] for j in range(n_dp)])
    full = jnp.concatenate([head, in_place], axis=1)
    grads = mm(full, xg, ((1,), (0,))).astype(bf16)

    def take(start, at):
        return grads[:, start : start + unit, at : at + width].reshape(hid, width)

    gate_grad = take(0, 0).T
    up_grad = take(unit, 0).T
    down_grad = take(2 * unit, width)
    layer_output, tokens_grad = call(
        functools.partial(combine_kernel, piece),
        [((block_len, piece), bf16), ((block_len, piece), bf16)],
        50_000_000,
        0,
        weight,
        place,
        place_b,
        place_c,
        back,
    )
    return layer_output, tokens_grad, gate_grad[None], up_grad[None], down_grad[None]


def solution(mesh):
    placed = (
        P("expert", "dp"),
        P("expert", None),
        P("expert", None),
        P("expert", "dp", "etp"),
        P("expert", "dp", "etp"),
        P("expert", "etp", "dp"),
        P("expert", "dp"),
    )
    return jax.shard_map(
        local,
        mesh=mesh,
        in_specs=placed,
        out_specs=(
            P("expert", ("dp", "etp")),
            P("expert", ("dp", "etp")),
            P("expert", "dp", "etp"),
            P("expert", "dp", "etp"),
            P("expert", "etp", "dp"),
        ),
        check_vma=False,
    )
```
